128 devices in a mesh: row: 8 (over x_lo, z), col: 16 (over x_hi, y, core).
Axes of the slice: x: 4 (x_hi: 2, x_lo: 2; x = x_hi * 2 + x_lo), y: 4, z: 4, core: 2. Of those that a mesh axis runs over, the one named last changes fastest.
Arguments:
- object_field: float32 [2, 8192, 16384], P(None, 'row', 'col'), may hold values from -6 to 6
- illumination: float32 [2, 128, 128], replicated, may hold values from -6 to 6
- positions: int32 [8, 16, 64, 2], P('row', 'col'), may hold values from 0 to 1023
- slot_counts: int32 [8, 16], P('row', 'col'), may hold values from 16 to 64, as said below
- amplitudes: float32 [8, 16, 64, 128, 128], P('row', 'col'), may hold values from 0.3 to 3
Outputs:
- object_new: float32 [2, 8192, 16384], P(None, 'row', 'col')
- probe_new: float32 [2, 128, 128], replicated
The draws below stay inside these ranges and needn't reach their ends.
Inputs may be any that keep to these rules, and one draw needn't show every extreme that they name: `slot_counts`: devices at the border of the mesh use at most 32 slots; some inner device uses all 64.
All inputs are finite; a program needn't handle non-finite values.
Results may differ from the reference program's by a relative error of at most 0.0003.
Values sent between devices are 32-bit elements; how exact they have to be, the bound alone decides.
A program may use at most 128 MiB of HBM per device.

```python
import math
import jax
import jax.numpy as jnp
from jax import lax

PATCH = 128
TILE = 1024
CAP = 64
NR = 8192
NC = 16384
N_ROW = 8
N_COL = 16


def draw_slot_counts(key, part):
    key = jax.random.fold_in(key, 11)
    key_counts, key_row, key_col = jax.random.split(key, 3)
    drawn_counts = jax.random.randint(key_counts, (N_ROW, N_COL), CAP // 4, CAP + 1)
    row_ids = jnp.arange(N_ROW)[:, None]
    col_ids = jnp.arange(N_COL)[None, :]
    border = (row_ids == 0) | (row_ids == N_ROW - 1) | (col_ids == 0) | (col_ids == N_COL - 1)
    drawn_counts = jnp.where(border, jnp.minimum(drawn_counts, CAP // 2), drawn_counts)
    pick_row = jax.random.randint(key_row, (), 1, N_ROW - 1)
    pick_col = jax.random.randint(key_col, (), 1, N_COL - 1)
    chosen = (row_ids == pick_row) & (col_ids == pick_col)
    return jnp.where(chosen, CAP, drawn_counts).astype(jnp.int32)


def place_ends(entries, key, least, largest):
    dims = entries.shape
    place = [jax.random.randint(jax.random.fold_in(key, axis), (), 0, dims[axis]) for axis in range(len(dims))]
    entries = entries.at[tuple(place)].set(least)
    longest = dims.index(max(dims))
    place[longest] = (place[longest] + 1) % dims[longest]
    return entries.at[tuple(place)].set(largest)


def levels(stream_key, dims, cuts, least, largest):
    level = 1.0
    for axis_at, parts in cuts:
        steps = jax.random.uniform(jax.random.fold_in(jax.random.fold_in(stream_key, 6), axis_at), (parts,), jnp.float32, least / len(cuts), largest / len(cuts))
        level = level * jnp.repeat(jnp.exp(steps), dims[axis_at] // parts).reshape((-1,) + (1,) * (len(dims) - 1 - axis_at))
    return level


def bell_draw(stream_key, extent, width, most, cuts=(), kind=jnp.bfloat16):
    entries = jax.random.normal(stream_key, extent, jnp.float32) * width
    if len(cuts) > 0:
        entries = levels(stream_key, extent, cuts, -0.22, 0.18) * entries
    return jnp.clip(entries, min=-most, max=most).astype(kind)


def setup_inputs(seed: int = 0) -> dict:
    splits = jax.random.split(jax.random.key(seed), 6)
    object_field = bell_draw(splits[0], (2, NR, NC), 1.0, 6.0, ((1, 8), (2, 16)), jnp.float32)
    illumination = bell_draw(splits[1], (2, PATCH, PATCH), 1.0, 6.0, (), jnp.float32)
    positions = place_ends(jax.random.randint(splits[2], (N_ROW, N_COL, CAP, 2), 0, TILE), jax.random.fold_in(splits[2], 1), 0, TILE - 1).astype(jnp.int32)
    slot_counts = draw_slot_counts(jax.random.fold_in(splits[5], 71), 0)
    amplitudes = jnp.clip(jnp.exp(math.log(3.0) - 2.3025851 * jax.random.uniform(splits[4], (N_ROW, N_COL, CAP, PATCH, PATCH), jnp.float32) ** levels(splits[4], (N_ROW, N_COL, CAP, PATCH, PATCH), ((0, 8), (1, 16)), -0.2, 0.2)), 0.3, 3.0)
    return dict(object_field=object_field, illumination=illumination, positions=positions, slot_counts=slot_counts, amplitudes=amplitudes)


floor_value = 0.5
step_object = 0.25


def reference(object_field, illumination, positions, slot_counts, amplitudes):
    half_width = PATCH // 2
    padded = jnp.pad(object_field, ((0, 0), (half_width, half_width), (half_width, half_width)))
    wave_probe = illumination[0] + 1j * illumination[1]
    slot_ids = jnp.arange(CAP, dtype=jnp.int32)

    def per_device(carry, device_id):
        gradient, probe_grad = carry
        row_id = device_id // N_COL
        col_id = device_id % N_COL
        offsets = positions[row_id, col_id]
        row_starts = (row_id * TILE + offsets[:, 0]).astype(jnp.int32)
        col_starts = (col_id * TILE + offsets[:, 1]).astype(jnp.int32)
        zero_index = jnp.int32(0)
        patches = jax.vmap(lambda row_start, col_start: lax.dynamic_slice(padded, (zero_index, row_start, col_start), (2, PATCH, PATCH)))(row_starts, col_starts)
        obj_wave = patches[:, 0] + 1j * patches[:, 1]
        exit_wave = wave_probe * obj_wave
        spectrum = jnp.fft.fft2(exit_wave, norm="ortho")
        modulus = jnp.abs(spectrum)
        projected = amplitudes[row_id, col_id] * spectrum / jnp.maximum(modulus, floor_value)
        revised = jnp.fft.ifft2(projected, norm="ortho")
        live = (slot_ids < slot_counts[row_id, col_id]).astype(object_field.dtype)
        change = (revised - exit_wave) * live[:, None, None]
        object_term = jnp.conj(wave_probe) * change
        probe_grad = probe_grad + jnp.sum(jnp.conj(obj_wave) * change, axis=0)
        terms = jnp.stack([object_term.real, object_term.imag], axis=1).astype(object_field.dtype)

        def add_slot(slot, grad_now):
            where = (zero_index, row_starts[slot], col_starts[slot])
            piece = lax.dynamic_slice(grad_now, where, (2, PATCH, PATCH))
            return lax.dynamic_update_slice(grad_now, piece + terms[slot], where)

        gradient = lax.fori_loop(0, CAP, add_slot, gradient)
        return (gradient, probe_grad), None

    start_grad = jnp.zeros_like(padded)
    start_probe = jnp.zeros((PATCH, PATCH), wave_probe.dtype)
    (gradient, probe_grad), _ = lax.scan(per_device, (start_grad, start_probe), jnp.arange(N_ROW * N_COL, dtype=jnp.int32))
    object_new = object_field + step_object * gradient[:, half_width:-half_width, half_width:-half_width]
    rate = (CAP * N_ROW * N_COL) ** -0.5
    probe_new = illumination + rate * jnp.stack([probe_grad.real, probe_grad.imag]).astype(illumination.dtype)
    return object_new, probe_new
```

```python
import functools
import math

import jax
import jax.numpy as jnp
import ml_dtypes
import numpy as np
from jax import lax
from jax.experimental import pallas as pl
from jax.experimental.pallas import tpu as pltpu
from jax.sharding import PartitionSpec as P

MESH = pl.DeviceIdType.MESH
PATCH = 128
HALF = 64
TILE = 1024
CAP = 64
LANE_TILES = TILE // PATCH
GROUP = 8
step_object = 0.25
DIRS = ((1, 0), (-1, 0), (0, 1), (0, -1), (1, 1), (1, -1), (-1, 1), (-1, -1))
SMALL_ROWS = 16
ANY = pl.BlockSpec(memory_space=pl.ANY)
IN_VMEM = pl.BlockSpec(memory_space=pltpu.VMEM)
IN_SMEM = pl.BlockSpec(memory_space=pltpu.SMEM)


def f32(*shape):
    return jax.ShapeDtypeStruct(shape, jnp.float32)


STRIPS = (
    f32(2, HALF, TILE), f32(2, HALF, TILE), f32(2, TILE, PATCH), f32(2, TILE, PATCH),
    f32(2, HALF, PATCH), f32(2, HALF, PATCH), f32(2, HALF, PATCH), f32(2, HALF, PATCH),
)


def tables():
    ids = np.arange(PATCH)
    angles = (np.outer(ids, ids) % PATCH) * (2 * math.pi / PATCH)
    cosine, sine = np.cos(angles) / math.sqrt(PATCH), np.sin(angles) / math.sqrt(PATCH)
    forward = np.block([[cosine, -sine], [sine, cosine]])
    out = []
    for matrix in (forward, forward.T):
        high = matrix.astype(np.float32).astype(ml_dtypes.bfloat16)
        out += [high, (matrix - high.astype(np.float64)).astype(np.float32).astype(ml_dtypes.bfloat16)]
    return np.stack(out)


def place():
    return lax.axis_index("row"), lax.axis_index("col"), lax.axis_size("row"), lax.axis_size("col")


def exists(da, db):
    a, b, rows, cols = place()
    return (a + da >= 0) & (a + da < rows) & (b + db >= 0) & (b + db < cols)


def strip_copy(d, src, dst, send_sem, recv_sem):
    a, b, _, _ = place()
    da, db = DIRS[d]
    return pltpu.make_async_remote_copy(
        src_ref=src, dst_ref=dst, send_sem=send_sem.at[d], recv_sem=recv_sem.at[d],
        device_id=(a + da, b + db), device_id_type=MESH,
    )


def start_strips(srcs, dsts, send_sem, recv_sem):
    for d, (da, db) in enumerate(DIRS):
        @pl.when(exists(da, db))
        def _():
            strip_copy(d, srcs[d], dsts[d], send_sem, recv_sem).start()


def wait_strips(srcs, dsts, send_sem, recv_sem):
    for d, (da, db) in enumerate(DIRS):
        @pl.when(exists(-da, -db))
        def _():
            strip_copy(d, srcs[d], dsts[d], send_sem, recv_sem).wait_recv()

        @pl.when(exists(da, db))
        def _():
            strip_copy(d, srcs[d], dsts[d], send_sem, recv_sem).wait_send()


def greet_strips(barrier, dirs):
    a, b, _, _ = place()
    for da, db in dirs:
        @pl.when(exists(da, db))
        def _():
            pl.semaphore_signal(barrier, inc=1, device_id=(a + da, b + db), device_id_type=MESH)


def halo_kernel(obj, *refs):
    strips, (send_sem, recv_sem) = refs[:8], refs[8:]
    a, b, rows, cols = place()
    barrier = pltpu.get_barrier_semaphore()
    greet_strips(barrier, DIRS)
    high = 1 + (a > 0).astype(jnp.int32) + (a < rows - 1).astype(jnp.int32)
    wide = 1 + (b > 0).astype(jnp.int32) + (b < cols - 1).astype(jnp.int32)
    pl.semaphore_wait(barrier, high * wide - 1)
    row_part = {1: slice(TILE - HALF, TILE), -1: slice(0, HALF), 0: slice(0, TILE)}
    col_part = {1: slice(TILE - PATCH, TILE), -1: slice(0, PATCH), 0: slice(0, TILE)}
    srcs = [obj.at[:, row_part[da], col_part[db]] for da, db in DIRS]
    start_strips(srcs, strips, send_sem, recv_sem)
    wait_strips(srcs, strips, send_sem, recv_sem)


def exchange_object(obj):
    return pl.pallas_call(
        halo_kernel,
        out_shape=STRIPS,
        in_specs=[ANY],
        out_specs=(ANY,) * 8,
        scratch_shapes=[pltpu.SemaphoreType.DMA((8,)), pltpu.SemaphoreType.DMA((8,))],
        compiler_params=pltpu.CompilerParams(collective_id=0, has_side_effects=True),
    )(obj)


def split(x):
    high = x.astype(jnp.bfloat16)
    return high, (x - high.astype(jnp.float32)).astype(jnp.bfloat16)


def dot(x, y):
    return jnp.dot(x, y, preferred_element_type=jnp.float32)


def right(x, high, low):
    xh, xl = split(x)
    return dot(xh, high) + dot(xl, high) + dot(xh, low)


def left(high, low, x):
    xh, xl = split(x)
    return dot(high, xh) + dot(high, xl) + dot(low, xh)


def border(d):
    da, db = DIRS[d]
    rows = {1: slice(0, HALF), -1: slice(HALF + TILE, 2 * HALF + TILE), 0: slice(HALF, HALF + TILE)}[da]
    return rows, {1: 0, -1: LANE_TILES + 1, 0: None}[db]


def border_views(buf, strip, d):
    rows, tile = border(d)
    if tile is not None:
        return [(strip, buf.at[:, tile, rows, :])]
    return [
        (strip.at[p, :, t * PATCH:(t + 1) * PATCH], buf.at[p, t + 1, rows, :])
        for p in range(2) for t in range(LANE_TILES)
    ]


def slots_kernel(pos, cnt, obj, ill, amp, tab, *refs):
    halo, out, edges, hout = refs[:8], refs[8], refs[9:17], refs[17]
    ob, gr, hacc, ampbuf, sem, asem, osem = refs[18:]
    count = cnt[0, 0]
    steps = (count + GROUP - 1) // GROUP
    body_copies = [
        pltpu.make_async_copy(obj.at[p, :, t * PATCH:(t + 1) * PATCH], ob.at[p, t + 1, HALF:HALF + TILE, :], sem.at[p * 8 + t])
        for p in range(2) for t in range(LANE_TILES)
    ]
    for copy in body_copies:
        copy.start()

    def amp_copy(i):
        return pltpu.make_async_copy(amp.at[0, 0, pl.ds(i * GROUP, GROUP)], ampbuf.at[i], asem.at[i])

    @pl.loop(0, steps)
    def _(i):
        amp_copy(i).start()

    halo_copies = []
    for d in range(8):
        views = border_views(ob, halo[d], d)
        halo_copies.append([pltpu.make_async_copy(src, dst, osem.at[d, n]) for n, (src, dst) in enumerate(views)])
    for d, (da, db) in enumerate(DIRS):
        @pl.when(exists(-da, -db))
        def _():
            for copy in halo_copies[d]:
                copy.start()

        @pl.when(jnp.logical_not(exists(-da, -db)))
        def _():
            rows, tile = border(d)
            for p in range(2):
                for t in range(1, LANE_TILES + 1) if tile is None else (tile,):
                    ob[p, t, rows, :] = jnp.zeros((rows.stop - rows.start, PATCH), jnp.float32)

    zero = jnp.zeros((PATCH, PATCH), jnp.float32)

    @pl.loop(0, (TILE + PATCH) // PATCH)
    def _(i):
        rows = pl.ds(pl.multiple_of(i * PATCH, PATCH), PATCH)
        for p in range(2):
            for t in range(LANE_TILES + 2):
                gr[p, t, rows, :] = zero
            ob[p, LANE_TILES + 2, rows, :] = zero
    hacc[...] = jnp.zeros_like(hacc)
    for copy in body_copies:
        copy.wait()
    for d, (da, db) in enumerate(DIRS):
        @pl.when(exists(-da, -db))
        def _():
            for copy in halo_copies[d]:
                copy.wait()
    lane = lax.broadcasted_iota(jnp.int32, (PATCH, PATCH), 1)

    def step(i, carry):
        amp_copy(i).wait()
        fh, fl, bh, bl = tab[0], tab[1], tab[2], tab[3]
        info, news = [], []
        for g in range(GROUP):
            s = i * GROUP + g
            live = s < count
            rows = pl.ds(pos[0, 0, s, 0], PATCH)
            column = pos[0, 0, s, 1] + HALF
            t, shift = column >> 7, column & (PATCH - 1)
            first = lane >= shift
            ta, tb = jnp.where(live, t, LANE_TILES + 2), jnp.where(live, t + 1, LANE_TILES + 2)
            o_r = jnp.where(first, ob[0, ta, rows, :], ob[0, tb, rows, :])
            o_i = jnp.where(first, ob[1, ta, rows, :], ob[1, tb, rows, :])
            p_r, p_i = pltpu.roll(ill[0], shift, 1), pltpu.roll(ill[1], shift, 1)
            info.append((rows, t, shift, first, o_r, o_i, p_r, p_i, p_r * o_r - p_i * o_i, p_r * o_i + p_i * o_r))
        for g in range(0, GROUP, 2):
            x = jnp.concatenate([jnp.concatenate(info[k][8:10], 1) for k in (g, g + 1)], 0)
            y = right(x, fh, fl)
            y = jnp.concatenate([jnp.concatenate([y[:PATCH, c:c + PATCH], y[PATCH:, c:c + PATCH]], 1) for c in (0, PATCH)], 0)
            z = left(bh, bl, y)
            z_r, z_i = z[:PATCH], z[PATCH:]
            a = jnp.concatenate([ampbuf[i, g], ampbuf[i, g + 1]], 1)
            factor = a * jnp.minimum(lax.rsqrt(z_r * z_r + z_i * z_i), 2.0)
            r = left(fh, fl, jnp.concatenate([factor * z_r, factor * z_i], 0))
            r = jnp.concatenate([jnp.concatenate([r[:PATCH, c:c + PATCH], r[PATCH:, c:c + PATCH]], 1) for c in (0, PATCH)], 0)
            n = right(r, bh, bl)
            news += [(n[:PATCH, :PATCH], n[:PATCH, PATCH:]), (n[PATCH:, :PATCH], n[PATCH:, PATCH:])]
        for g in range(GROUP):
            rows, t, shift, first, o_r, o_i, p_r, p_i, w_r, w_i = info[g]
            c_r, c_i = news[g][0] - w_r, news[g][1] - w_i
            for p, term in ((0, p_r * c_r + p_i * c_i), (1, p_r * c_i - p_i * c_r)):
                now = jnp.where(first, gr[p, t, rows, :], gr[p, t + 1, rows, :]) + term
                pltpu.store(gr.at[p, t, rows, :], now, mask=first)
                pltpu.store(gr.at[p, t + 1, rows, :], now, mask=jnp.logical_not(first))
            back = PATCH - shift
            hacc[0:PATCH] += pltpu.roll(o_r * c_r + o_i * c_i, back, 1)
            hacc[PATCH:] += pltpu.roll(o_r * c_i - o_i * c_r, back, 1)
        return carry

    lax.fori_loop(0, steps, step, 0)
    hout[...] = hacc[...]
    last = []
    for d in range(8):
        da, db = DIRS[d]
        views = border_views(gr, edges[d], DIRS.index((-da, -db)))
        last += [pltpu.make_async_copy(dst, src, osem.at[d, n]) for n, (src, dst) in enumerate(views)]
    for copy in last:
        copy.start()
    for p in range(2):
        for t in range(LANE_TILES):
            @pl.loop(0, TILE // PATCH)
            def _(i):
                rows = pl.ds(pl.multiple_of(HALF + i * PATCH, HALF), PATCH)
                ob[p, t + 1, rows, :] += step_object * gr[p, t + 1, rows, :]
            copy = pltpu.make_async_copy(
                ob.at[p, t + 1, HALF:HALF + TILE, :], out.at[p, :, t * PATCH:(t + 1) * PATCH], sem.at[p * 8 + t])
            copy.start()
            last.append(copy)
    for copy in last:
        copy.wait()


def run_slots(positions, slot_counts, obj, ill, amplitudes, halo):
    return pl.pallas_call(
        slots_kernel,
        out_shape=(f32(2, TILE, TILE),) + STRIPS + (f32(2 * PATCH, PATCH),),
        in_specs=[IN_SMEM, IN_SMEM, ANY, IN_VMEM, ANY, IN_VMEM] + [ANY] * 8,
        out_specs=(ANY,) * 9 + (IN_VMEM,),
        scratch_shapes=[
            pltpu.VMEM((2, LANE_TILES + 3, TILE + PATCH, PATCH), jnp.float32),
            pltpu.VMEM((2, LANE_TILES + 2, TILE + PATCH, PATCH), jnp.float32),
            pltpu.VMEM((2 * PATCH, PATCH), jnp.float32),
            pltpu.VMEM((CAP // GROUP, GROUP, PATCH, PATCH), jnp.float32),
            pltpu.SemaphoreType.DMA((16,)), pltpu.SemaphoreType.DMA((CAP // GROUP,)), pltpu.SemaphoreType.DMA((8, 16)),
        ],
        compiler_params=pltpu.CompilerParams(vmem_limit_bytes=50 * 2**20),
    )(positions, slot_counts, obj, ill, amplitudes, jnp.asarray(tables()), *halo)


def return_kernel(h, *refs):
    edges, strips, total = refs[:8], refs[8:16], refs[16]
    pieces, sums, gathered, send_sem, recv_sem, s1, r1, s2, r2, s3, r3 = refs[17:]
    a, b, rows, cols = place()
    barrier = pltpu.get_barrier_semaphore()
    greet_strips(barrier, DIRS[4:])

    def col_peer(k):
        return lax.rem(b + k, cols)

    def row_peer(k):
        return lax.rem(a + k, rows)

    @pl.loop(1, cols)
    def _(k):
        pl.semaphore_signal(barrier, inc=1, device_id=(a, col_peer(k)), device_id_type=MESH)

    @pl.loop(1, rows)
    def _(k):
        pl.semaphore_signal(barrier, inc=1, device_id=(row_peer(k), b), device_id_type=MESH)

    high = (a > 0).astype(jnp.int32) + (a < rows - 1).astype(jnp.int32)
    wide = (b > 0).astype(jnp.int32) + (b < cols - 1).astype(jnp.int32)
    pl.semaphore_wait(barrier, cols - 1 + rows - 1 + high * wide)

    def piece_rows(k):
        return pl.ds(pl.multiple_of(k * SMALL_ROWS, SMALL_ROWS), SMALL_ROWS)

    def scatter(peer, slot):
        return pltpu.make_async_remote_copy(
            src_ref=h.at[piece_rows(peer)], dst_ref=pieces.at[slot], send_sem=s1.at[peer], recv_sem=r1.at[slot],
            device_id=(a, peer), device_id_type=MESH)

    def share(peer, slot):
        return pltpu.make_async_remote_copy(
            src_ref=sums.at[slot], dst_ref=sums.at[slot], send_sem=s2.at[peer], recv_sem=r2.at[slot],
            device_id=(peer, b), device_id_type=MESH)

    def gather(peer, slot):
        return pltpu.make_async_remote_copy(
            src_ref=gathered.at[slot], dst_ref=gathered.at[slot], send_sem=s3.at[peer], recv_sem=r3.at[slot],
            device_id=(a, peer), device_id_type=MESH)

    @pl.loop(1, cols)
    def _(k):
        scatter(col_peer(k), b).start()

    start_strips(edges, strips, send_sem, recv_sem)
    pieces[b] = h[piece_rows(b), :]

    @pl.loop(1, cols)
    def _(k):
        scatter(b, col_peer(k)).wait_recv()

    sums[a] = jnp.sum(pieces[...], axis=0)

    @pl.loop(1, rows)
    def _(k):
        share(row_peer(k), a).start()

    @pl.loop(1, rows)
    def _(k):
        share(a, row_peer(k)).wait_recv()

    gathered[b] = jnp.sum(sums[...], axis=0)

    @pl.loop(1, cols)
    def _(k):
        gather(col_peer(k), b).start()

    @pl.loop(1, cols)
    def _(k):
        gather(b, col_peer(k)).wait_recv()

    total[...] = gathered[...]

    @pl.loop(1, cols)
    def _(k):
        scatter(col_peer(k), b).wait_send()
        gather(col_peer(k), b).wait_send()

    @pl.loop(1, rows)
    def _(k):
        share(row_peer(k), a).wait_send()

    wait_strips(edges, strips, send_sem, recv_sem)


def return_edges(h, edges):
    rows, cols = lax.axis_size("row"), lax.axis_size("col")
    dma = pltpu.SemaphoreType.DMA
    return pl.pallas_call(
        return_kernel,
        out_shape=STRIPS + (f32(cols, SMALL_ROWS, PATCH),),
        in_specs=[IN_VMEM] + [ANY] * 8,
        out_specs=(ANY,) * 8 + (IN_VMEM,),
        scratch_shapes=[
            pltpu.VMEM((cols, SMALL_ROWS, PATCH), jnp.float32), pltpu.VMEM((rows, SMALL_ROWS, PATCH), jnp.float32),
            pltpu.VMEM((cols, SMALL_ROWS, PATCH), jnp.float32), dma((8,)), dma((8,)),
            dma((cols,)), dma((cols,)), dma((rows,)), dma((rows,)), dma((cols,)), dma((cols,)),
        ],
        compiler_params=pltpu.CompilerParams(collective_id=1, has_side_effects=True),
    )(h, *edges)


def finish_kernel(rate, core, ill, total, *refs):
    strips, out, probe = refs[:8], refs[8], refs[9]
    top, bottom, west, east, sem = refs[10:]
    inner = slice(HALF, TILE - HALF)
    parts = (
        (top, out.at[:, 0:HALF, :]), (bottom, out.at[:, TILE - HALF:TILE, :]),
        (west, out.at[:, inner, 0:PATCH]), (east, out.at[:, inner, TILE - PATCH:TILE]),
    )
    reads = [pltpu.make_async_copy(hbm, vmem, sem.at[n]) for n, (vmem, hbm) in enumerate(parts)]
    writes = [pltpu.make_async_copy(vmem, hbm, sem.at[n]) for n, (vmem, hbm) in enumerate(parts)]
    for copy in reads:
        copy.start()
    probe[...] = ill[...] + rate * total[...]
    for copy in reads:
        copy.wait()
    lo, hi = slice(0, PATCH), slice(TILE - PATCH, TILE)
    adds = (
        ((top, slice(None), slice(None), slice(None)),),
        ((bottom, slice(None), slice(None), slice(None)),),
        ((west, slice(None), slice(None), inner), (top, slice(None), lo, slice(0, HALF)), (bottom, slice(None), lo, slice(TILE - HALF, TILE))),
        ((east, slice(None), slice(None), inner), (top, slice(None), hi, slice(0, HALF)), (bottom, slice(None), hi, slice(TILE - HALF, TILE))),
        ((top, slice(None), lo, slice(None)),), ((top, slice(None), hi, slice(None)),),
        ((bottom, slice(None), lo, slice(None)),), ((bottom, slice(None), hi, slice(None)),),
    )
    for d, (da, db) in enumerate(DIRS):
        @pl.when(exists(-da, -db))
        def _():
            for target, rows, cols, source in adds[d]:
                target[:, rows, cols] += step_object * strips[d][:, source, :]
    for copy in writes:
        copy.start()
    for copy in writes:
        copy.wait()


def finish(core, ill, total, strips):
    rate = (CAP * lax.axis_size("row") * lax.axis_size("col")) ** (-0.5)
    return pl.pallas_call(
        functools.partial(finish_kernel, rate),
        out_shape=(f32(2, TILE, TILE), f32(2, PATCH, PATCH)),
        in_specs=[ANY, IN_VMEM, IN_VMEM] + [IN_VMEM] * 8,
        out_specs=(ANY, IN_VMEM),
        input_output_aliases={0: 0},
        scratch_shapes=[
            pltpu.VMEM((2, HALF, TILE), jnp.float32), pltpu.VMEM((2, HALF, TILE), jnp.float32),
            pltpu.VMEM((2, TILE - PATCH, PATCH), jnp.float32), pltpu.VMEM((2, TILE - PATCH, PATCH), jnp.float32),
            pltpu.SemaphoreType.DMA((4,)),
        ],
        compiler_params=pltpu.CompilerParams(vmem_limit_bytes=32 * 2**20),
    )(core, ill, total.reshape(2, PATCH, PATCH), *strips)


def shards(object_field, illumination, positions, slot_counts, amplitudes):
    halo = exchange_object(object_field)
    core, *rest = run_slots(positions, slot_counts, object_field, illumination, amplitudes, halo)
    edges, h = rest[:8], rest[8]
    *strips, total = return_edges(h, edges)
    return finish(core, illumination, total, strips)


def solution(mesh):
    placed = (
        P(None, "row", "col"),
        P(),
        P("row", "col", None, None),
        P("row", "col"),
        P("row", "col", None, None, None),
    )
    return jax.shard_map(
        shards, mesh=mesh, in_specs=placed, out_specs=(P(None, "row", "col"), P()), check_vma=False
    )
```

```python
import functools
import math

import jax
import jax.numpy as jnp
import ml_dtypes
import numpy as np
from jax import lax
from jax.experimental import pallas as pl
from jax.experimental.pallas import tpu as pltpu
from jax.sharding import PartitionSpec as P

MESH = pl.DeviceIdType.MESH
PATCH = 128
HALF = 64
TILE = 1024
CAP = 64
LANE_TILES = TILE // PATCH
GROUP = 8
GROUP_FAR = 4
RING = 8
step_object = 0.25
DIRS = ((1, 0), (-1, 0), (0, 1), (0, -1), (1, 1), (1, -1), (-1, 1), (-1, -1))
SMALL_ROWS = 32
ANY = pl.BlockSpec(memory_space=pltpu.HBM)
IN_VMEM = pl.BlockSpec(memory_space=pltpu.VMEM)
IN_SMEM = pl.BlockSpec(memory_space=pltpu.SMEM)


def f32(*shape):
    return jax.ShapeDtypeStruct(shape, jnp.float32)


STRIPS = (
    f32(2, HALF, TILE), f32(2, HALF, TILE), f32(2, TILE // 2, PATCH), f32(2, TILE // 2, PATCH),
    f32(2, HALF, PATCH), f32(2, HALF, PATCH), f32(2, HALF, PATCH), f32(2, HALF, PATCH),
)


def tables():
    ids = np.arange(PATCH)
    angles = (np.outer(ids, ids) % PATCH) * (2 * math.pi / PATCH)
    cosine, sine = np.cos(angles) / math.sqrt(PATCH), np.sin(angles) / math.sqrt(PATCH)
    forward = np.block([[cosine, -sine], [sine, cosine]])
    out = []
    for matrix in (forward, forward.T):
        high = matrix.astype(np.float32).astype(ml_dtypes.bfloat16)
        out += [high, (matrix - high.astype(np.float64)).astype(np.float32).astype(ml_dtypes.bfloat16)]
    return np.stack(out)


def place():
    return lax.axis_index("row"), lax.axis_index("col"), lax.axis_size("row"), lax.axis_size("col")


def exists(da, db):
    a, b, rows, cols = place()
    return (a + da >= 0) & (a + da < rows) & (b + db >= 0) & (b + db < cols)


def strip_copy(d, src, dst, send_sem, recv_sem):
    a, b, _, _ = place()
    da, db = DIRS[d]
    return pltpu.make_async_remote_copy(
        src_ref=src, dst_ref=dst, send_sem=send_sem.at[d], recv_sem=recv_sem.at[d],
        device_id=(a + da, b + db), device_id_type=MESH,
    )


def start_strips(srcs, dsts, send_sem, recv_sem, which=range(8)):
    for d in which:
        da, db = DIRS[d]

        @pl.when(exists(da, db))
        def _():
            strip_copy(d, srcs[d], dsts[d], send_sem, recv_sem).start()


def wait_strips(srcs, dsts, send_sem, recv_sem):
    for d, (da, db) in enumerate(DIRS):
        @pl.when(exists(-da, -db))
        def _():
            strip_copy(d, srcs[d], dsts[d], send_sem, recv_sem).wait_recv()

        @pl.when(exists(da, db))
        def _():
            strip_copy(d, srcs[d], dsts[d], send_sem, recv_sem).wait_send()


def greet_strips(barrier, dirs):
    a, b, _, _ = place()
    for da, db in dirs:
        @pl.when(exists(da, db))
        def _():
            pl.semaphore_signal(barrier, inc=1, device_id=(a + da, b + db), device_id_type=MESH)


def folded(low_lanes, first, second):
    keep = (lax.broadcasted_iota(jnp.int32, first.shape, 1) < HALF) == low_lanes
    return jnp.where(keep, first, pltpu.roll(second, HALF, 1))


def split(x):
    high = x.astype(jnp.bfloat16)
    return high, (x - high.astype(jnp.float32)).astype(jnp.bfloat16)


def dot(x, y):
    return jnp.dot(x, y, preferred_element_type=jnp.float32)


def right(xs, high, low):
    parts = [split(x) for x in xs]
    both = dot(jnp.concatenate([half for part in parts for half in part], 0), high)
    rest = dot(jnp.concatenate([part[0] for part in parts], 0), low)
    n = xs[0].shape[0]
    return [both[2 * n * k:2 * n * k + n] + both[2 * n * k + n:2 * n * (k + 1)] + rest[n * k:n * (k + 1)] for k in range(len(xs))]


def left(high, low, x):
    xh, xl = split(x)
    return dot(high, xh) + dot(high, xl) + dot(low, xh)


def side_by_side(y):
    return jnp.concatenate([jnp.concatenate([y[:PATCH, c:c + PATCH], y[PATCH:, c:c + PATCH]], 1) for c in (0, PATCH)], 0)


def project(z, a):
    z_r, z_i = z[:PATCH], z[PATCH:]
    factor = a * jnp.minimum(lax.rsqrt(z_r * z_r + z_i * z_i), 2.0)
    return jnp.concatenate([factor * z_r, factor * z_i], 0)


def solve(waves, amps, tab):
    fh, fl, bh, bl = tab[0], tab[1], tab[2], tab[3]
    xs = [jnp.concatenate([jnp.concatenate(waves[k], 1) for k in (g, g + 1)], 0) for g in range(0, len(waves), 2)]
    ys = right(xs, fh, fl)
    qs = [project(left(bh, bl, side_by_side(y)), a) for y, a in zip(ys, amps)]
    ns = right([side_by_side(left(fh, fl, q)) for q in qs], bh, bl)
    return [(n[r:r + PATCH, :PATCH], n[r:r + PATCH, PATCH:]) for n in ns for r in (0, PATCH)]


def patch_wave(buf, ill, rows, ta, tb, shift, first):
    o_r = jnp.where(first, buf[0, ta, rows, :], buf[0, tb, rows, :])
    o_i = jnp.where(first, buf[1, ta, rows, :], buf[1, tb, rows, :])
    p_r, p_i = pltpu.roll(ill[0], shift, 1), pltpu.roll(ill[1], shift, 1)
    return (o_r, o_i, p_r, p_i), (p_r * o_r - p_i * o_i, p_r * o_i + p_i * o_r)


def gradients(parts, wave, new):
    o_r, o_i, p_r, p_i = parts
    c_r, c_i = new[0] - wave[0], new[1] - wave[1]
    terms = (p_r * c_r + p_i * c_i, p_r * c_i - p_i * c_r)
    return terms, (o_r * c_r + o_i * c_i, o_r * c_i - o_i * c_r)


def inside(row, column):
    return (row >= HALF) & (row <= TILE - HALF) & (column >= HALF) & (column <= TILE - HALF)


def early_kernel(pos, cnt, obj, ill, amp, tab, *refs):
    strips, terms, hout = refs[:8], refs[8], refs[9]
    ob, packed, staged, hacc, ampbuf, sem, asem, tsem, send_sem, recv_sem = refs[10:]
    a, b, rows, cols = place()
    count = cnt[0, 0]
    steps = CAP // GROUP
    barrier = pltpu.get_barrier_semaphore()
    greet_strips(barrier, DIRS)
    order = (LANE_TILES - 1, 0) + tuple(range(1, LANE_TILES - 1))
    reads = {
        (p, t): pltpu.make_async_copy(obj.at[p, :, t * PATCH:(t + 1) * PATCH], ob.at[p, t], sem.at[p * LANE_TILES + t])
        for t in order for p in range(2)
    }
    for copy in reads.values():
        copy.start()

    def amp_copy(i):
        return pltpu.make_async_copy(amp.at[0, 0, pl.ds(i * GROUP, GROUP)], ampbuf.at[i], asem.at[i])

    for i in range(steps):
        amp_copy(i).start()
    high = 1 + (a > 0).astype(jnp.int32) + (a < rows - 1).astype(jnp.int32)
    wide = 1 + (b > 0).astype(jnp.int32) + (b < cols - 1).astype(jnp.int32)
    pl.semaphore_wait(barrier, high * wide - 1)
    row_part = {1: slice(TILE - HALF, TILE), -1: slice(0, HALF), 0: slice(0, TILE)}
    col_part = {1: slice(TILE - PATCH, TILE), -1: slice(0, PATCH), 0: slice(0, TILE)}
    srcs = [obj.at[:, row_part[da], col_part[db]] for da, db in DIRS]
    srcs[2], srcs[3] = packed.at[0], packed.at[1]
    start_strips(srcs, strips, send_sem, recv_sem, (0, 1, 4, 5, 6, 7))
    half = TILE // 2
    for n, t in enumerate((LANE_TILES - 1, 0)):
        for p in range(2):
            reads[p, t].wait()
            packed[n, p] = folded(n == 1, ob[p, t, 0:half, :], ob[p, t, half:TILE, :])
        start_strips(srcs, strips, send_sem, recv_sem, (2 + n,))
    for p in range(2):
        ob[p, LANE_TILES] = jnp.zeros((TILE, PATCH), jnp.float32)
    hacc[...] = jnp.zeros_like(hacc)
    for t in order[2:]:
        for p in range(2):
            reads[p, t].wait()
    lane = lax.broadcasted_iota(jnp.int32, (PATCH, PATCH), 1)

    def term_copy(i):
        return pltpu.make_async_copy(staged.at[lax.rem(i, 2)], terms.at[pl.ds(i * GROUP, GROUP)], tsem.at[lax.rem(i, 2)])

    def step(i, carry):
        amp_copy(i).wait()
        info, waves = [], []
        for g in range(GROUP):
            s = i * GROUP + g
            row, column = pos[0, 0, s, 0], pos[0, 0, s, 1]
            good = inside(row, column) & (s < count)
            start = jnp.where(good, row - HALF, 0)
            at = jnp.where(good, column - HALF, 0)
            t, shift = at >> 7, at & (PATCH - 1)
            ta = jnp.where(good, t, LANE_TILES)
            tb = jnp.where(good, jnp.minimum(t + 1, LANE_TILES - 1), LANE_TILES)
            parts, wave = patch_wave(ob, ill, pl.ds(start, PATCH), ta, tb, shift, lane >= shift)
            info.append((parts, shift))
            waves.append(wave)
        amps = [jnp.concatenate([ampbuf[i, g], ampbuf[i, g + 1]], 1) for g in range(0, GROUP, 2)]
        news = solve(waves, amps, tab)

        @pl.when(i >= 2)
        def _():
            term_copy(i - 2).wait()
        for g in range(GROUP):
            parts, shift = info[g]
            out, h = gradients(parts, waves[g], news[g])
            for p in range(2):
                staged[lax.rem(i, 2), g, p] = out[p]
                hacc[p * PATCH:(p + 1) * PATCH] += pltpu.roll(h[p], PATCH - shift, 1)
        term_copy(i).start()
        return carry

    lax.fori_loop(0, steps, step, 0)
    hout[...] = hacc[...]
    for i in (steps - 2, steps - 1):
        term_copy(i).wait()
    wait_strips(srcs, strips, send_sem, recv_sem)


def run_early(positions, slot_counts, obj, ill, amplitudes, tab):
    dma = pltpu.SemaphoreType.DMA
    return pl.pallas_call(
        early_kernel,
        out_shape=STRIPS + (f32(CAP, 2, PATCH, PATCH), f32(2 * PATCH, PATCH)),
        in_specs=[IN_SMEM, IN_SMEM, ANY, IN_VMEM, ANY, IN_VMEM],
        out_specs=(ANY,) * 9 + (IN_VMEM,),
        scratch_shapes=[
            pltpu.VMEM((2, LANE_TILES + 1, TILE, PATCH), jnp.float32), pltpu.VMEM((2, 2, TILE // 2, PATCH), jnp.float32),
            pltpu.VMEM((2, GROUP, 2, PATCH, PATCH), jnp.float32), pltpu.VMEM((2 * PATCH, PATCH), jnp.float32),
            pltpu.VMEM((CAP // GROUP, GROUP, PATCH, PATCH), jnp.float32),
            dma((2 * LANE_TILES,)), dma((CAP // GROUP,)), dma((2,)), dma((8,)), dma((8,)),
        ],
        compiler_params=pltpu.CompilerParams(collective_id=0, has_side_effects=True, vmem_limit_bytes=58 * 2**20),
    )(positions, slot_counts, obj, ill, amplitudes, tab)


def border(d):
    da, db = DIRS[d]
    rows = {1: slice(0, HALF), -1: slice(HALF + TILE, 2 * HALF + TILE), 0: slice(HALF, HALF + TILE)}[da]
    return rows, {1: 0, -1: LANE_TILES + 1, 0: None}[db]


def border_views(buf, strip, d):
    rows, tile = border(d)
    if DIRS[d][0] == 0:
        return [(strip, buf.at[:, tile, HALF:HALF + TILE // 2, :])]
    if tile is not None:
        return [(strip, buf.at[:, tile, rows, :])]
    return [
        (strip.at[p, :, t * PATCH:(t + 1) * PATCH], buf.at[p, t + 1, rows, :])
        for p in range(2) for t in range(LANE_TILES)
    ]


def slots_kernel(pos, cnt, obj, ill, amp, tab, terms, hearly, *refs):
    halo, out, edges, hout = refs[:8], refs[8], refs[9:17], refs[17]
    ob, gr, hacc, ampbuf, held, near, far, sem, asem, tsem, osem = refs[18:]
    count = cnt[0, 0]
    body_copies = [
        pltpu.make_async_copy(obj.at[p, :, t * PATCH:(t + 1) * PATCH], ob.at[p, t + 1, HALF:HALF + TILE, :], sem.at[p * 8 + t])
        for p in range(2) for t in range(LANE_TILES)
    ]

    def listed(s, sizes):
        good = inside(pos[0, 0, s, 0], pos[0, 0, s, 1])

        @pl.when(good)
        def _():
            near[sizes[0]] = s

        @pl.when(jnp.logical_not(good))
        def _():
            far[sizes[1]] = s
        step = good.astype(jnp.int32)
        return sizes[0] + step, sizes[1] + 1 - step

    n_near, n_far = lax.fori_loop(0, count, listed, (jnp.int32(0), jnp.int32(0)))

    def term_copy(j):
        return pltpu.make_async_copy(terms.at[near[j]], held.at[lax.rem(j, RING)], tsem.at[lax.rem(j, RING)])

    def amp_copy(j):
        return pltpu.make_async_copy(amp.at[0, 0, far[j]], ampbuf.at[j], asem.at[j])

    @pl.loop(0, jnp.minimum(n_near, RING))
    def _(j):
        term_copy(j).start()

    @pl.loop(0, n_far)
    def _(j):
        amp_copy(j).start()

    for copy in body_copies:
        copy.start()
    halo_copies = []
    for d in range(8):
        views = border_views(ob, halo[d], d)
        halo_copies.append([pltpu.make_async_copy(src, dst, osem.at[d, n]) for n, (src, dst) in enumerate(views)])
    for d, (da, db) in enumerate(DIRS):
        @pl.when(exists(-da, -db))
        def _():
            for copy in halo_copies[d]:
                copy.start()

        @pl.when(jnp.logical_not(exists(-da, -db)))
        def _():
            rows, tile = border(d)
            for p in range(2):
                for t in range(1, LANE_TILES + 1) if tile is None else (tile,):
                    ob[p, t, rows, :] = jnp.zeros((rows.stop - rows.start, PATCH), jnp.float32)

    zero = jnp.zeros((PATCH, PATCH), jnp.float32)

    @pl.loop(0, (TILE + PATCH) // PATCH)
    def _(i):
        rows = pl.ds(pl.multiple_of(i * PATCH, PATCH), PATCH)
        for p in range(2):
            for t in range(LANE_TILES + 2):
                gr[p, t, rows, :] = zero
            ob[p, LANE_TILES + 2, rows, :] = zero
    hacc[...] = hearly[...]
    lane = lax.broadcasted_iota(jnp.int32, (PATCH, PATCH), 1)

    def add(rows, t, first, term):
        for p in range(2):
            now = jnp.where(first, gr[p, t, rows, :], gr[p, t + 1, rows, :]) + term[p]
            pltpu.store(gr.at[p, t, rows, :], now, mask=first)
            pltpu.store(gr.at[p, t + 1, rows, :], now, mask=jnp.logical_not(first))

    @pl.loop(0, n_near)
    def _(j):
        s = near[j]
        term_copy(j).wait()
        column = pos[0, 0, s, 1] + HALF
        add(pl.ds(pos[0, 0, s, 0], PATCH), column >> 7, lane >= (column & (PATCH - 1)), [held[lax.rem(j, RING), p] for p in range(2)])

        @pl.when(j + RING < n_near)
        def _():
            term_copy(j + RING).start()

    for copy in body_copies:
        copy.wait()
    for d, (da, db) in enumerate(DIRS):
        @pl.when(exists(-da, -db))
        def _():
            for copy in halo_copies[d]:
                copy.wait()
            if da == 0:
                tile = border(d)[1]
                for p in range(2):
                    ob[p, tile, HALF + TILE // 2:HALF + TILE, :] = pltpu.roll(ob[p, tile, HALF:HALF + TILE // 2, :], HALF, 1)

    @pl.loop(0, n_far)
    def _(j):
        amp_copy(j).wait()

    def step(i, carry):
        info, waves, slots = [], [], []
        for g in range(GROUP_FAR):
            live = i * GROUP_FAR + g < n_far
            j = jnp.where(live, i * GROUP_FAR + g, 0)
            s = far[j]
            rows = pl.ds(pos[0, 0, s, 0], PATCH)
            column = pos[0, 0, s, 1] + HALF
            t, shift = column >> 7, column & (PATCH - 1)
            first = lane >= shift
            ta, tb = jnp.where(live, t, LANE_TILES + 2), jnp.where(live, t + 1, LANE_TILES + 2)
            parts, wave = patch_wave(ob, ill, rows, ta, tb, shift, first)
            info.append((rows, t, shift, first, parts))
            waves.append(wave)
            slots.append(j)
        amps = [jnp.concatenate([ampbuf[slots[g]], ampbuf[slots[g + 1]]], 1) for g in range(0, GROUP_FAR, 2)]
        news = solve(waves, amps, tab)
        for g in range(GROUP_FAR):
            rows, t, shift, first, parts = info[g]
            term, h = gradients(parts, waves[g], news[g])
            add(rows, t, first, term)
            for p in range(2):
                hacc[p * PATCH:(p + 1) * PATCH] += pltpu.roll(h[p], PATCH - shift, 1)
        return carry

    lax.fori_loop(0, (n_far + GROUP_FAR - 1) // GROUP_FAR, step, 0)
    hout[...] = hacc[...]
    last = []
    for tile in (0, LANE_TILES + 1):
        for p in range(2):
            gr[p, tile, HALF:HALF + TILE // 2, :] = folded(
                tile > 0, gr[p, tile, HALF:HALF + TILE // 2, :], gr[p, tile, HALF + TILE // 2:HALF + TILE, :])
    for d in range(8):
        da, db = DIRS[d]
        views = border_views(gr, edges[d], DIRS.index((-da, -db)))
        last += [pltpu.make_async_copy(dst, src, osem.at[d, n]) for n, (src, dst) in enumerate(views)]
    for copy in last:
        copy.start()
    for p in range(2):
        for t in range(LANE_TILES):
            @pl.loop(0, TILE // PATCH)
            def _(i):
                rows = pl.ds(pl.multiple_of(HALF + i * PATCH, HALF), PATCH)
                ob[p, t + 1, rows, :] += step_object * gr[p, t + 1, rows, :]
            copy = pltpu.make_async_copy(
                ob.at[p, t + 1, HALF:HALF + TILE, :], out.at[p, :, t * PATCH:(t + 1) * PATCH], sem.at[p * 8 + t])
            copy.start()
            last.append(copy)
    for copy in last:
        copy.wait()


def run_slots(positions, slot_counts, obj, ill, amplitudes, tab, terms, hearly, halo):
    dma = pltpu.SemaphoreType.DMA
    return pl.pallas_call(
        slots_kernel,
        out_shape=(f32(2, TILE, TILE),) + STRIPS + (f32(2 * PATCH, PATCH),),
        in_specs=[IN_SMEM, IN_SMEM, ANY, IN_VMEM, ANY, IN_VMEM, ANY, IN_VMEM] + [ANY] * 8,
        out_specs=(ANY,) * 9 + (IN_VMEM,),
        scratch_shapes=[
            pltpu.VMEM((2, LANE_TILES + 3, TILE + PATCH, PATCH), jnp.float32),
            pltpu.VMEM((2, LANE_TILES + 2, TILE + PATCH, PATCH), jnp.float32),
            pltpu.VMEM((2 * PATCH, PATCH), jnp.float32), pltpu.VMEM((CAP, PATCH, PATCH), jnp.float32),
            pltpu.VMEM((RING, 2, PATCH, PATCH), jnp.float32), pltpu.SMEM((CAP,), jnp.int32), pltpu.SMEM((CAP,), jnp.int32),
            dma((16,)), dma((CAP,)), dma((RING,)), dma((8, 16)),
        ],
        compiler_params=pltpu.CompilerParams(vmem_limit_bytes=58 * 2**20),
    )(positions, slot_counts, obj, ill, amplitudes, tab, terms, hearly, *halo)


def return_kernel(h, *refs):
    edges, strips, total = refs[:8], refs[8:16], refs[16]
    pieces, sums, gathered, send_sem, recv_sem, s1, r1, s2, r2, s3, r3 = refs[17:]
    a, b, rows, cols = place()
    barrier = pltpu.get_barrier_semaphore()
    greet_strips(barrier, DIRS[4:])

    def col_peer(k):
        return lax.rem(b + k, cols)

    def row_peer(k):
        return lax.rem(a + k, rows)

    for k in range(1, rows):
        pl.semaphore_signal(barrier, inc=1, device_id=(row_peer(k), b), device_id_type=MESH)
    for k in range(1, cols):
        pl.semaphore_signal(barrier, inc=1, device_id=(a, col_peer(k)), device_id_type=MESH)
    high = (a > 0).astype(jnp.int32) + (a < rows - 1).astype(jnp.int32)
    wide = (b > 0).astype(jnp.int32) + (b < cols - 1).astype(jnp.int32)
    pl.semaphore_wait(barrier, cols - 1 + rows - 1 + high * wide)

    def piece_rows(k):
        return pl.ds(pl.multiple_of(k * SMALL_ROWS, SMALL_ROWS), SMALL_ROWS)

    def scatter(peer, slot):
        return pltpu.make_async_remote_copy(
            src_ref=h.at[piece_rows(peer)], dst_ref=pieces.at[slot], send_sem=s1.at[peer], recv_sem=r1.at[slot],
            device_id=(peer, b), device_id_type=MESH)

    def share(peer, slot):
        return pltpu.make_async_remote_copy(
            src_ref=sums.at[slot], dst_ref=sums.at[slot], send_sem=s2.at[peer], recv_sem=r2.at[slot],
            device_id=(a, peer), device_id_type=MESH)

    def gather(peer, slot):
        return pltpu.make_async_remote_copy(
            src_ref=gathered.at[slot], dst_ref=gathered.at[slot], send_sem=s3.at[peer], recv_sem=r3.at[slot],
            device_id=(peer, b), device_id_type=MESH)

    for k in range(1, rows):
        scatter(row_peer(k), a).start()
    start_strips(edges, strips, send_sem, recv_sem)
    pieces[a] = h[piece_rows(a), :]
    for k in range(1, rows):
        scatter(a, row_peer(k)).wait_recv()
    sums[b] = jnp.sum(pieces[...], axis=0)
    for k in range(1, cols):
        share(col_peer(k), b).start()
    for k in range(1, cols):
        share(b, col_peer(k)).wait_recv()
    gathered[a] = jnp.sum(sums[...], axis=0)
    for k in range(1, rows):
        gather(row_peer(k), a).start()
    for k in range(1, rows):
        gather(a, row_peer(k)).wait_recv()
    total[...] = gathered[...]
    for k in range(1, rows):
        scatter(row_peer(k), a).wait_send()
        gather(row_peer(k), a).wait_send()
    for k in range(1, cols):
        share(col_peer(k), b).wait_send()
    wait_strips(edges, strips, send_sem, recv_sem)


def return_edges(h, edges):
    rows, cols = lax.axis_size("row"), lax.axis_size("col")
    dma = pltpu.SemaphoreType.DMA
    return pl.pallas_call(
        return_kernel,
        out_shape=STRIPS + (f32(rows, SMALL_ROWS, PATCH),),
        in_specs=[IN_VMEM] + [ANY] * 8,
        out_specs=(ANY,) * 8 + (IN_VMEM,),
        scratch_shapes=[
            pltpu.VMEM((rows, SMALL_ROWS, PATCH), jnp.float32), pltpu.VMEM((cols, SMALL_ROWS, PATCH), jnp.float32),
            pltpu.VMEM((rows, SMALL_ROWS, PATCH), jnp.float32), dma((8,)), dma((8,)),
            dma((rows,)), dma((rows,)), dma((cols,)), dma((cols,)), dma((rows,)), dma((rows,)),
        ],
        compiler_params=pltpu.CompilerParams(collective_id=1, has_side_effects=True, vmem_limit_bytes=58 * 2**20),
    )(h, *edges)


def finish_kernel(rate, core, ill, total, *refs):
    strips, out, probe = refs[:8], refs[8], refs[9]
    top, bottom, west, east, sem, strip_sem = refs[10:16]
    held = refs[16:]
    middle = slice(HALF, TILE - HALF)
    parts = (
        (top, out.at[:, 0:HALF, :]), (bottom, out.at[:, TILE - HALF:TILE, :]),
        (west, out.at[:, middle, 0:PATCH]), (east, out.at[:, middle, TILE - PATCH:TILE]),
    )
    reads = [pltpu.make_async_copy(hbm, vmem, sem.at[n]) for n, (vmem, hbm) in enumerate(parts)]
    writes = [pltpu.make_async_copy(vmem, hbm, sem.at[n]) for n, (vmem, hbm) in enumerate(parts)]
    fetches = [pltpu.make_async_copy(strips[d], held[d], strip_sem.at[d]) for d in range(8)]
    for copy in reads:
        copy.start()
    for d, (da, db) in enumerate(DIRS):
        @pl.when(exists(-da, -db))
        def _():
            fetches[d].start()
    probe[...] = ill[...] + rate * total[...]
    for copy in reads:
        copy.wait()
    half = TILE // 2
    for d, (da, db) in enumerate(DIRS):
        @pl.when(exists(-da, -db))
        def _():
            fetches[d].wait()
            if da != 0:
                target = top if da > 0 else bottom
                cols = {0: slice(0, TILE), 1: slice(0, PATCH), -1: slice(TILE - PATCH, TILE)}[db]
                target[:, :, cols] += step_object * held[d][...]
            else:
                side = west if db > 0 else east
                cols = slice(0, PATCH) if db > 0 else slice(TILE - PATCH, TILE)
                low = lax.broadcasted_iota(jnp.int32, (half, PATCH), 1) < HALF
                keep = low if db > 0 else jnp.logical_not(low)
                for p in range(2):
                    first = jnp.where(keep, step_object * held[d][p], 0.0)
                    second = jnp.where(keep, pltpu.roll(step_object * held[d][p], HALF, 1), 0.0)
                    top[p, :, cols] += first[0:HALF]
                    side[p, 0:half - HALF, :] += first[HALF:half]
                    side[p, half - HALF:TILE - PATCH, :] += second[0:half - HALF]
                    bottom[p, :, cols] += second[half - HALF:half]
    for copy in writes:
        copy.start()
    for copy in writes:
        copy.wait()


def finish(core, ill, total, strips):
    rate = (CAP * lax.axis_size("row") * lax.axis_size("col")) ** (-0.5)
    return pl.pallas_call(
        functools.partial(finish_kernel, rate),
        out_shape=(f32(2, TILE, TILE), f32(2, PATCH, PATCH)),
        in_specs=[ANY, IN_VMEM, IN_VMEM] + [ANY] * 8,
        out_specs=(ANY, IN_VMEM),
        input_output_aliases={0: 0},
        scratch_shapes=[
            pltpu.VMEM((2, HALF, TILE), jnp.float32), pltpu.VMEM((2, HALF, TILE), jnp.float32),
            pltpu.VMEM((2, TILE - PATCH, PATCH), jnp.float32), pltpu.VMEM((2, TILE - PATCH, PATCH), jnp.float32),
            pltpu.SemaphoreType.DMA((4,)), pltpu.SemaphoreType.DMA((8,)),
        ] + [pltpu.VMEM(strip.shape, jnp.float32) for strip in STRIPS],
        compiler_params=pltpu.CompilerParams(vmem_limit_bytes=58 * 2**20),
    )(core, ill, total.reshape(2, PATCH, PATCH), *strips)


def shards(object_field, illumination, positions, slot_counts, amplitudes):
    shared = (positions, slot_counts, object_field, illumination, amplitudes, jnp.asarray(tables()))
    *halo, terms, hearly = run_early(*shared)
    core, *rest = run_slots(*shared, terms, hearly, halo)
    edges, h = rest[:8], rest[8]
    *strips, total = return_edges(h, edges)
    return finish(core, illumination, total, strips)


def solution(mesh):
    placed = (
        P(None, "row", "col"),
        P(),
        P("row", "col", None, None),
        P("row", "col"),
        P("row", "col", None, None, None),
    )
    return jax.shard_map(
        shards, mesh=mesh, in_specs=placed, out_specs=(P(None, "row", "col"), P()), check_vma=False
    )
```

```python
import functools
import math

import jax
import jax.numpy as jnp
import ml_dtypes
import numpy as np
from jax import lax
from jax.experimental import pallas as pl
from jax.experimental.pallas import tpu as pltpu
from jax.sharding import PartitionSpec as P

MESH = pl.DeviceIdType.MESH
PATCH = 128
HALF = 64
TILE = 1024
CAP = 64
LANE_TILES = TILE // PATCH
GROUP = 16
GROUP_FAR = 4
CHUNKS = 4
PACE = (0, 0, 1, 2, 4)
RING = 8
step_object = 0.25
DIRS = ((1, 0), (-1, 0), (0, 1), (0, -1), (1, 1), (1, -1), (-1, 1), (-1, -1))
SMALL_ROWS = 16
ANY = pl.BlockSpec(memory_space=pltpu.HBM)
IN_VMEM = pl.BlockSpec(memory_space=pltpu.VMEM)
IN_SMEM = pl.BlockSpec(memory_space=pltpu.SMEM)


def f32(*shape):
    return jax.ShapeDtypeStruct(shape, jnp.float32)


STRIPS = (
    f32(2, HALF, TILE), f32(2, HALF, TILE), f32(2, TILE // 2, PATCH), f32(2, TILE // 2, PATCH),
    f32(2, HALF, PATCH), f32(2, HALF, PATCH), f32(2, HALF, PATCH), f32(2, HALF, PATCH),
)


def tables():
    ids = np.arange(PATCH)
    angles = (np.outer(ids, ids) % PATCH) * (2 * math.pi / PATCH)
    cosine, sine = np.cos(angles) / math.sqrt(PATCH), np.sin(angles) / math.sqrt(PATCH)
    forward = np.block([[cosine, -sine], [sine, cosine]])
    out = []
    for matrix in (forward, forward.T):
        high = matrix.astype(np.float32).astype(ml_dtypes.bfloat16)
        out += [high, (matrix - high.astype(np.float64)).astype(np.float32).astype(ml_dtypes.bfloat16)]
    return np.stack(out)


def place():
    return lax.axis_index("row"), lax.axis_index("col"), lax.axis_size("row"), lax.axis_size("col")


def exists(da, db):
    a, b, rows, cols = place()
    return (a + da >= 0) & (a + da < rows) & (b + db >= 0) & (b + db < cols)


def strip_copy(d, src, dst, send_sem, recv_sem):
    a, b, _, _ = place()
    da, db = DIRS[d]
    return pltpu.make_async_remote_copy(
        src_ref=src, dst_ref=dst, send_sem=send_sem.at[d], recv_sem=recv_sem.at[d],
        device_id=(a + da, b + db), device_id_type=MESH,
    )


def start_strips(srcs, dsts, send_sem, recv_sem, which=range(8)):
    for d in which:
        da, db = DIRS[d]

        @pl.when(exists(da, db))
        def _():
            strip_copy(d, srcs[d], dsts[d], send_sem, recv_sem).start()


def wait_strips(srcs, dsts, send_sem, recv_sem, which=range(8)):
    for d in which:
        da, db = DIRS[d]

        @pl.when(exists(-da, -db))
        def _():
            strip_copy(d, srcs[d], dsts[d], send_sem, recv_sem).wait_recv()

        @pl.when(exists(da, db))
        def _():
            strip_copy(d, srcs[d], dsts[d], send_sem, recv_sem).wait_send()


def greet_strips(barrier, dirs):
    a, b, _, _ = place()
    for da, db in dirs:
        @pl.when(exists(da, db))
        def _():
            pl.semaphore_signal(barrier, inc=1, device_id=(a + da, b + db), device_id_type=MESH)


def folded(low_lanes, first, second):
    keep = (lax.broadcasted_iota(jnp.int32, first.shape, 1) < HALF) == low_lanes
    return jnp.where(keep, first, pltpu.roll(second, HALF, 1))


def split(x):
    high = x.astype(jnp.bfloat16)
    return high, (x - high.astype(jnp.float32)).astype(jnp.bfloat16)


def dot(x, y):
    return jnp.dot(x, y, preferred_element_type=jnp.float32)


def right(xs, high, low):
    parts = [split(x) for x in xs]
    both = dot(jnp.concatenate([half for part in parts for half in part], 0), high)
    rest = dot(jnp.concatenate([part[0] for part in parts], 0), low)
    n = xs[0].shape[0]
    return [both[2 * n * k:2 * n * k + n] + both[2 * n * k + n:2 * n * (k + 1)] + rest[n * k:n * (k + 1)] for k in range(len(xs))]


def left(high, low, x):
    xh, xl = split(x)
    return dot(high, xh) + dot(high, xl) + dot(low, xh)


def side_by_side(y):
    return jnp.concatenate([jnp.concatenate([y[:PATCH, c:c + PATCH], y[PATCH:, c:c + PATCH]], 1) for c in (0, PATCH)], 0)


def project(z, a):
    z_r, z_i = z[:PATCH], z[PATCH:]
    factor = a * jnp.minimum(lax.rsqrt(z_r * z_r + z_i * z_i), 2.0)
    return jnp.concatenate([factor * z_r, factor * z_i], 0)


def solve(waves, amps, tab):
    fh, fl, bh, bl = tab[0], tab[1], tab[2], tab[3]
    pairs = range(len(waves) // 2)
    held = [jnp.concatenate([jnp.concatenate(waves[k], 1) for k in (2 * p, 2 * p + 1)], 0) for p in pairs]
    cut = len(pairs) // 2
    for tick in range(5):
        for stage, part in ((tick, list(pairs[:cut])), (tick - 1, list(pairs[cut:]))):
            if stage in (0, 3):
                done = right([held[p] for p in part], *((fh, fl) if stage == 0 else (bh, bl)))
            elif stage == 1:
                done = [project(left(bh, bl, side_by_side(held[p])), amps[p]) for p in part]
            elif stage == 2:
                done = [side_by_side(left(fh, fl, held[p])) for p in part]
            else:
                continue
            for p, value in zip(part, done):
                held[p] = value
    return [(n[r:r + PATCH, :PATCH], n[r:r + PATCH, PATCH:]) for n in held for r in (0, PATCH)]


def patch_wave(buf, ill, rows, ta, tb, shift, first):
    o_r = jnp.where(first, buf[0, ta, rows, :], buf[0, tb, rows, :])
    o_i = jnp.where(first, buf[1, ta, rows, :], buf[1, tb, rows, :])
    p_r, p_i = pltpu.roll(ill[0], shift, 1), pltpu.roll(ill[1], shift, 1)
    return (o_r, o_i, p_r, p_i), (p_r * o_r - p_i * o_i, p_r * o_i + p_i * o_r)


def gradients(parts, wave, new):
    o_r, o_i, p_r, p_i = parts
    c_r, c_i = new[0] - wave[0], new[1] - wave[1]
    terms = (p_r * c_r + p_i * c_i, p_r * c_i - p_i * c_r)
    return terms, (o_r * c_r + o_i * c_i, o_r * c_i - o_i * c_r)


def inside(row, column):
    return (row >= HALF) & (row <= TILE - HALF) & (column >= HALF) & (column <= TILE - HALF)


def early_kernel(pos, cnt, obj, ill, amp, tab, *refs):
    strips, terms, hout = refs[:8], refs[8], refs[9]
    ob, packed, staged, hacc, ampbuf, sem, asem, tsem, send_sem, recv_sem = refs[10:]
    a, b, rows, cols = place()
    count = cnt[0, 0]
    steps = CAP // GROUP
    barrier = pltpu.get_barrier_semaphore()
    greet_strips(barrier, DIRS)
    order = (LANE_TILES - 1, 0) + tuple(range(1, LANE_TILES - 1))
    reads = {
        (p, t): pltpu.make_async_copy(obj.at[p, :, t * PATCH:(t + 1) * PATCH], ob.at[p, t], sem.at[p * LANE_TILES + t])
        for t in order for p in range(2)
    }
    for copy in reads.values():
        copy.start()

    def amp_copy(i):
        return pltpu.make_async_copy(amp.at[0, 0, pl.ds(i * GROUP, GROUP)], ampbuf.at[i], asem.at[i])

    for i in range(steps):
        amp_copy(i).start()
    high = 1 + (a > 0).astype(jnp.int32) + (a < rows - 1).astype(jnp.int32)
    wide = 1 + (b > 0).astype(jnp.int32) + (b < cols - 1).astype(jnp.int32)
    pl.semaphore_wait(barrier, high * wide - 1)
    row_part = {1: slice(TILE - HALF, TILE), -1: slice(0, HALF), 0: slice(0, TILE)}
    col_part = {1: slice(TILE - PATCH, TILE), -1: slice(0, PATCH), 0: slice(0, TILE)}
    srcs = [obj.at[:, row_part[da], col_part[db]] for da, db in DIRS]
    srcs[2], srcs[3] = packed.at[0], packed.at[1]
    start_strips(srcs, strips, send_sem, recv_sem, (0, 1, 4, 5, 6, 7))
    half = TILE // 2
    for n, t in enumerate((LANE_TILES - 1, 0)):
        for p in range(2):
            reads[p, t].wait()
            packed[n, p] = folded(n == 1, ob[p, t, 0:half, :], ob[p, t, half:TILE, :])
        start_strips(srcs, strips, send_sem, recv_sem, (2 + n,))
    for p in range(2):
        ob[p, LANE_TILES] = jnp.zeros((TILE, PATCH), jnp.float32)
    hacc[...] = jnp.zeros_like(hacc)
    for t in order[2:]:
        for p in range(2):
            reads[p, t].wait()
    lane = lax.broadcasted_iota(jnp.int32, (PATCH, PATCH), 1)

    def term_copy(i):
        return pltpu.make_async_copy(staged.at[lax.rem(i, 2)], terms.at[pl.ds(i * GROUP, GROUP)], tsem.at[lax.rem(i, 2)])

    def step(i, carry):
        amp_copy(i).wait()
        info, waves = [], []
        for g in range(GROUP):
            s = i * GROUP + g
            row, column = pos[0, 0, 0, s], pos[0, 0, 1, s]
            good = inside(row, column) & (s < count)
            start = jnp.where(good, row - HALF, 0)
            at = jnp.where(good, column - HALF, 0)
            t, shift = at >> 7, at & (PATCH - 1)
            ta = jnp.where(good, t, LANE_TILES)
            tb = jnp.where(good, jnp.minimum(t + 1, LANE_TILES - 1), LANE_TILES)
            parts, wave = patch_wave(ob, ill, pl.ds(start, PATCH), ta, tb, shift, lane >= shift)
            info.append((parts, shift))
            waves.append(wave)
        amps = [jnp.concatenate([ampbuf[i, g], ampbuf[i, g + 1]], 1) for g in range(0, GROUP, 2)]
        news = solve(waves, amps, tab)

        @pl.when(i >= 2)
        def _():
            term_copy(i - 2).wait()
        for g in range(GROUP):
            parts, shift = info[g]
            out, h = gradients(parts, waves[g], news[g])
            for p in range(2):
                staged[lax.rem(i, 2), g, p] = out[p]
                hacc[p * PATCH:(p + 1) * PATCH] += pltpu.roll(h[p], PATCH - shift, 1)
        term_copy(i).start()
        return carry

    lax.fori_loop(0, steps, step, 0)
    hout[...] = hacc[...]
    for i in (steps - 2, steps - 1):
        term_copy(i).wait()
    wait_strips(srcs, strips, send_sem, recv_sem)


def run_early(positions, slot_counts, obj, ill, amplitudes, tab):
    dma = pltpu.SemaphoreType.DMA
    return pl.pallas_call(
        early_kernel,
        out_shape=STRIPS + (f32(CAP, 2, PATCH, PATCH), f32(2 * PATCH, PATCH)),
        in_specs=[IN_SMEM, IN_SMEM, ANY, IN_VMEM, ANY, IN_VMEM],
        out_specs=(ANY,) * 9 + (IN_VMEM,),
        scratch_shapes=[
            pltpu.VMEM((2, LANE_TILES + 1, TILE, PATCH), jnp.float32), pltpu.VMEM((2, 2, TILE // 2, PATCH), jnp.float32),
            pltpu.VMEM((2, GROUP, 2, PATCH, PATCH), jnp.float32), pltpu.VMEM((2 * PATCH, PATCH), jnp.float32),
            pltpu.VMEM((CAP // GROUP, GROUP, PATCH, PATCH), jnp.float32),
            dma((2 * LANE_TILES,)), dma((CAP // GROUP,)), dma((2,)), dma((8,)), dma((8,)),
        ],
        compiler_params=pltpu.CompilerParams(collective_id=0, has_side_effects=True, vmem_limit_bytes=58 * 2**20),
    )(positions, slot_counts, obj, ill, amplitudes, tab)


def border(d):
    da, db = DIRS[d]
    rows = {1: slice(0, HALF), -1: slice(HALF + TILE, 2 * HALF + TILE), 0: slice(HALF, HALF + TILE)}[da]
    return rows, {1: 0, -1: LANE_TILES + 1, 0: None}[db]


def border_views(buf, strip, d):
    rows, tile = border(d)
    if DIRS[d][0] == 0:
        return [(strip, buf.at[:, tile, HALF:HALF + TILE // 2, :])]
    if tile is not None:
        return [(strip, buf.at[:, tile, rows, :])]
    return [
        (strip.at[p, :, t * PATCH:(t + 1) * PATCH], buf.at[p, t + 1, rows, :])
        for p in range(2) for t in range(LANE_TILES)
    ]


def slots_kernel(pos, cnt, obj, ill, amp, tab, terms, hearly, *refs):
    halo, out, edges, hout = refs[:8], refs[8], refs[9:17], refs[17]
    ob, gr, hacc, ampbuf, held, near, far, sem, asem, tsem, osem = refs[18:]
    count = cnt[0, 0]
    body_copies = [
        pltpu.make_async_copy(obj.at[p, :, t * PATCH:(t + 1) * PATCH], ob.at[p, t + 1, HALF:HALF + TILE, :], sem.at[p * 8 + t])
        for p in range(2) for t in range(LANE_TILES)
    ]

    def listed(s, sizes):
        good = inside(pos[0, 0, 0, s], pos[0, 0, 1, s])

        @pl.when(good)
        def _():
            near[sizes[0]] = s

        @pl.when(jnp.logical_not(good))
        def _():
            far[sizes[1]] = s
        step = good.astype(jnp.int32)
        return sizes[0] + step, sizes[1] + 1 - step

    n_near, n_far = lax.fori_loop(0, count, listed, (jnp.int32(0), jnp.int32(0)))

    def term_copy(j):
        return pltpu.make_async_copy(terms.at[near[j]], held.at[lax.rem(j, RING)], tsem.at[lax.rem(j, RING)])

    def amp_copy(j):
        return pltpu.make_async_copy(amp.at[0, 0, far[j]], ampbuf.at[j], asem.at[j])

    @pl.loop(0, jnp.minimum(n_near, RING))
    def _(j):
        term_copy(j).start()

    @pl.loop(0, n_far)
    def _(j):
        amp_copy(j).start()

    for copy in body_copies:
        copy.start()
    halo_copies = []
    for d in range(8):
        views = border_views(ob, halo[d], d)
        halo_copies.append([pltpu.make_async_copy(src, dst, osem.at[d, n]) for n, (src, dst) in enumerate(views)])
    for d, (da, db) in enumerate(DIRS):
        @pl.when(exists(-da, -db))
        def _():
            for copy in halo_copies[d]:
                copy.start()

        @pl.when(jnp.logical_not(exists(-da, -db)))
        def _():
            rows, tile = border(d)
            for p in range(2):
                for t in range(1, LANE_TILES + 1) if tile is None else (tile,):
                    ob[p, t, rows, :] = jnp.zeros((rows.stop - rows.start, PATCH), jnp.float32)

    zero = jnp.zeros((PATCH, PATCH), jnp.float32)

    @pl.loop(0, (TILE + PATCH) // PATCH)
    def _(i):
        rows = pl.ds(pl.multiple_of(i * PATCH, PATCH), PATCH)
        for p in range(2):
            for t in range(LANE_TILES + 2):
                gr[p, t, rows, :] = zero
            ob[p, LANE_TILES + 2, rows, :] = zero
    hacc[...] = hearly[...]
    lane = lax.broadcasted_iota(jnp.int32, (PATCH, PATCH), 1)

    def add(rows, t, first, term):
        for p in range(2):
            now = jnp.where(first, gr[p, t, rows, :], gr[p, t + 1, rows, :]) + term[p]
            pltpu.store(gr.at[p, t, rows, :], now, mask=first)
            pltpu.store(gr.at[p, t + 1, rows, :], now, mask=jnp.logical_not(first))

    @pl.loop(0, n_near)
    def _(j):
        s = near[j]
        term_copy(j).wait()
        column = pos[0, 0, 1, s] + HALF
        add(pl.ds(pos[0, 0, 0, s], PATCH), column >> 7, lane >= (column & (PATCH - 1)), [held[lax.rem(j, RING), p] for p in range(2)])

        @pl.when(j + RING < n_near)
        def _():
            term_copy(j + RING).start()

    for copy in body_copies:
        copy.wait()
    for d, (da, db) in enumerate(DIRS):
        @pl.when(exists(-da, -db))
        def _():
            for copy in halo_copies[d]:
                copy.wait()
            if da == 0:
                tile = border(d)[1]
                for p in range(2):
                    ob[p, tile, HALF + TILE // 2:HALF + TILE, :] = pltpu.roll(ob[p, tile, HALF:HALF + TILE // 2, :], HALF, 1)

    @pl.loop(0, n_far)
    def _(j):
        amp_copy(j).wait()

    def step(i, carry):
        info, waves, slots = [], [], []
        for g in range(GROUP_FAR):
            live = i * GROUP_FAR + g < n_far
            j = jnp.where(live, i * GROUP_FAR + g, 0)
            s = far[j]
            rows = pl.ds(pos[0, 0, 0, s], PATCH)
            column = pos[0, 0, 1, s] + HALF
            t, shift = column >> 7, column & (PATCH - 1)
            first = lane >= shift
            ta, tb = jnp.where(live, t, LANE_TILES + 2), jnp.where(live, t + 1, LANE_TILES + 2)
            parts, wave = patch_wave(ob, ill, rows, ta, tb, shift, first)
            info.append((rows, t, shift, first, parts))
            waves.append(wave)
            slots.append(j)
        amps = [jnp.concatenate([ampbuf[slots[g]], ampbuf[slots[g + 1]]], 1) for g in range(0, GROUP_FAR, 2)]
        news = solve(waves, amps, tab)
        for g in range(GROUP_FAR):
            rows, t, shift, first, parts = info[g]
            term, h = gradients(parts, waves[g], news[g])
            add(rows, t, first, term)
            for p in range(2):
                hacc[p * PATCH:(p + 1) * PATCH] += pltpu.roll(h[p], PATCH - shift, 1)
        return carry

    lax.fori_loop(0, (n_far + GROUP_FAR - 1) // GROUP_FAR, step, 0)
    hout[...] = hacc[...]
    last = []
    for tile in (0, LANE_TILES + 1):
        for p in range(2):
            gr[p, tile, HALF:HALF + TILE // 2, :] = folded(
                tile > 0, gr[p, tile, HALF:HALF + TILE // 2, :], gr[p, tile, HALF + TILE // 2:HALF + TILE, :])
    for d in range(8):
        da, db = DIRS[d]
        views = border_views(gr, edges[d], DIRS.index((-da, -db)))
        last += [pltpu.make_async_copy(dst, src, osem.at[d, n]) for n, (src, dst) in enumerate(views)]
    for copy in last:
        copy.start()
    for p in range(2):
        for t in range(LANE_TILES):
            @pl.loop(0, TILE // PATCH)
            def _(i):
                rows = pl.ds(pl.multiple_of(HALF + i * PATCH, HALF), PATCH)
                ob[p, t + 1, rows, :] += step_object * gr[p, t + 1, rows, :]
            copy = pltpu.make_async_copy(
                ob.at[p, t + 1, HALF:HALF + TILE, :], out.at[p, :, t * PATCH:(t + 1) * PATCH], sem.at[p * 8 + t])
            copy.start()
            last.append(copy)
    for copy in last:
        copy.wait()


def run_slots(positions, slot_counts, obj, ill, amplitudes, tab, terms, hearly, halo):
    dma = pltpu.SemaphoreType.DMA
    return pl.pallas_call(
        slots_kernel,
        out_shape=(f32(2, TILE, TILE),) + STRIPS + (f32(2 * PATCH, PATCH),),
        in_specs=[IN_SMEM, IN_SMEM, ANY, IN_VMEM, ANY, IN_VMEM, ANY, IN_VMEM] + [ANY] * 8,
        out_specs=(ANY,) * 9 + (IN_VMEM,),
        scratch_shapes=[
            pltpu.VMEM((2, LANE_TILES + 3, TILE + PATCH, PATCH), jnp.float32),
            pltpu.VMEM((2, LANE_TILES + 2, TILE + PATCH, PATCH), jnp.float32),
            pltpu.VMEM((2 * PATCH, PATCH), jnp.float32), pltpu.VMEM((CAP, PATCH, PATCH), jnp.float32),
            pltpu.VMEM((RING, 2, PATCH, PATCH), jnp.float32), pltpu.SMEM((CAP,), jnp.int32), pltpu.SMEM((CAP,), jnp.int32),
            dma((16,)), dma((CAP,)), dma((RING,)), dma((8, 16)),
        ],
        compiler_params=pltpu.CompilerParams(vmem_limit_bytes=58 * 2**20),
    )(positions, slot_counts, obj, ill, amplitudes, tab, terms, hearly, *halo)


def return_kernel(h, *refs):
    edges, strips, total = refs[:8], refs[8:16], refs[16]
    other, mine, pieces, sums, gathered, send_sem, recv_sem, s0, r0, s1, r1, s2, r2, s3, r3 = refs[17:]
    a, b, rows, cols = place()
    chips = cols // 2
    q, core = b // 2, lax.rem(b, 2)
    partner = (a, b + 1 - 2 * core)

    def row_peer(k):
        return lax.rem(a + k, rows)

    def chip_peer(k):
        return lax.rem(q + k, chips)

    barrier = pltpu.get_barrier_semaphore()
    greet_strips(barrier, DIRS[4:])
    pl.semaphore_signal(barrier, inc=1, device_id=partner, device_id_type=MESH)
    for k in range(1, rows):
        pl.semaphore_signal(barrier, inc=1, device_id=(row_peer(k), b), device_id_type=MESH)
    for k in range(1, chips):
        pl.semaphore_signal(barrier, inc=1, device_id=(a, chip_peer(k) * 2 + core), device_id_type=MESH)
    across = ((core == 1) & (b < cols - 1)) | ((core == 0) & (b > 0))
    side = b + 2 * core - 1

    @pl.when(across)
    def _():
        pl.semaphore_signal(barrier, inc=1, device_id=(a, side), device_id_type=MESH)
    high = (a > 0).astype(jnp.int32) + (a < rows - 1).astype(jnp.int32)
    wide = (b > 0).astype(jnp.int32) + (b < cols - 1).astype(jnp.int32)
    pl.semaphore_wait(barrier, 1 + rows - 1 + chips - 1 + across.astype(jnp.int32) + high * wide)

    def piece_rows(k):
        return pl.ds(pl.multiple_of(k * SMALL_ROWS, SMALL_ROWS), SMALL_ROWS)

    def half_rows(k):
        return pl.ds(pl.multiple_of(k * PATCH, PATCH), PATCH)

    def remote(src, dst, send, recv, device):
        return pltpu.make_async_remote_copy(
            src_ref=src, dst_ref=dst, send_sem=send, recv_sem=recv, device_id=device, device_id_type=MESH)

    def swap():
        return remote(h.at[half_rows(1 - core)], other, s0.at[0], r0.at[0], partner)

    def scatter(peer, slot):
        return remote(mine.at[piece_rows(peer)], pieces.at[slot], s1.at[peer], r1.at[slot], (peer, b))

    def share(peer, slot):
        return remote(sums.at[slot], sums.at[slot], s2.at[peer], r2.at[slot], (a, peer * 2 + core))

    def gather(peer, slot):
        return remote(gathered.at[core, slot], gathered.at[core, slot], s3.at[peer], r3.at[slot], (peer, b))

    def hand(which):
        return remote(gathered.at[which], gathered.at[which], s0.at[1], r0.at[1], partner)

    def parts(refs, c):
        return [
            ref if d >= 4 else ref.at[:, c * (HALF // CHUNKS):(c + 1) * (HALF // CHUNKS), :] if d < 2
            else ref.at[:, c * (TILE // 2 // CHUNKS):(c + 1) * (TILE // 2 // CHUNKS), :]
            for d, ref in enumerate(refs)
        ]

    def send_strips(stage):
        for c in range(PACE[stage], PACE[stage + 1]):
            start_strips(parts(edges, c), parts(strips, c), send_sem.at[c], recv_sem.at[c], range(8) if c == 0 else range(4))

    swap().start()
    send_strips(0)
    swap().wait_recv()
    mine[...] = h[half_rows(core), :] + other[...]
    for k in range(1, rows):
        scatter(row_peer(k), a).start()
    send_strips(1)
    pieces[a] = mine[piece_rows(a), :]
    for k in range(1, rows):
        scatter(a, row_peer(k)).wait_recv()
    sums[q] = jnp.sum(pieces[...], axis=0)
    for k in range(1, chips):
        share(chip_peer(k), q).start()
    send_strips(2)
    for k in range(1, chips):
        share(q, chip_peer(k)).wait_recv()
    gathered[core, a] = jnp.sum(sums[...], axis=0)
    for k in range(1, rows):
        gather(row_peer(k), a).start()
    send_strips(3)
    for k in range(1, rows):
        gather(a, row_peer(k)).wait_recv()
    hand(core).start()
    hand(1 - core).wait_recv()
    total[...] = gathered[...]
    swap().wait_send()
    hand(core).wait_send()
    for k in range(1, rows):
        scatter(row_peer(k), a).wait_send()
        gather(row_peer(k), a).wait_send()
    for k in range(1, chips):
        share(chip_peer(k), q).wait_send()
    for c in range(CHUNKS):
        wait_strips(parts(edges, c), parts(strips, c), send_sem.at[c], recv_sem.at[c], range(8) if c == 0 else range(4))


def return_edges(h, edges):
    rows, chips = lax.axis_size("row"), lax.axis_size("col") // 2
    dma = pltpu.SemaphoreType.DMA
    return pl.pallas_call(
        return_kernel,
        out_shape=STRIPS + (f32(2, rows, SMALL_ROWS, PATCH),),
        in_specs=[IN_VMEM] + [ANY] * 8,
        out_specs=(ANY,) * 8 + (IN_VMEM,),
        scratch_shapes=[
            pltpu.VMEM((PATCH, PATCH), jnp.float32), pltpu.VMEM((PATCH, PATCH), jnp.float32),
            pltpu.VMEM((rows, SMALL_ROWS, PATCH), jnp.float32), pltpu.VMEM((chips, SMALL_ROWS, PATCH), jnp.float32),
            pltpu.VMEM((2, rows, SMALL_ROWS, PATCH), jnp.float32), dma((CHUNKS, 8)), dma((CHUNKS, 8)),
            dma((2,)), dma((2,)), dma((rows,)), dma((rows,)), dma((chips,)), dma((chips,)), dma((rows,)), dma((rows,)),
        ],
        compiler_params=pltpu.CompilerParams(collective_id=1, has_side_effects=True, vmem_limit_bytes=58 * 2**20),
    )(h, *edges)


def finish_kernel(rate, core, ill, total, *refs):
    strips, out, probe = refs[:8], refs[8], refs[9]
    top, bottom, west, east, sem, strip_sem = refs[10:16]
    held = refs[16:]
    middle = slice(HALF, TILE - HALF)
    parts = (
        (top, out.at[:, 0:HALF, :]), (bottom, out.at[:, TILE - HALF:TILE, :]),
        (west, out.at[:, middle, 0:PATCH]), (east, out.at[:, middle, TILE - PATCH:TILE]),
    )
    reads = [pltpu.make_async_copy(hbm, vmem, sem.at[n]) for n, (vmem, hbm) in enumerate(parts)]
    writes = [pltpu.make_async_copy(vmem, hbm, sem.at[n]) for n, (vmem, hbm) in enumerate(parts)]
    fetches = [pltpu.make_async_copy(strips[d], held[d], strip_sem.at[d]) for d in range(8)]
    for copy in reads:
        copy.start()
    for d, (da, db) in enumerate(DIRS):
        @pl.when(exists(-da, -db))
        def _():
            fetches[d].start()
    probe[...] = ill[...] + rate * total[...]
    for copy in reads:
        copy.wait()
    half = TILE // 2
    for d, (da, db) in enumerate(DIRS):
        @pl.when(exists(-da, -db))
        def _():
            fetches[d].wait()
            if da != 0:
                target = top if da > 0 else bottom
                cols = {0: slice(0, TILE), 1: slice(0, PATCH), -1: slice(TILE - PATCH, TILE)}[db]
                target[:, :, cols] += step_object * held[d][...]
            else:
                side = west if db > 0 else east
                cols = slice(0, PATCH) if db > 0 else slice(TILE - PATCH, TILE)
                low = lax.broadcasted_iota(jnp.int32, (half, PATCH), 1) < HALF
                keep = low if db > 0 else jnp.logical_not(low)
                for p in range(2):
                    first = jnp.where(keep, step_object * held[d][p], 0.0)
                    second = jnp.where(keep, pltpu.roll(step_object * held[d][p], HALF, 1), 0.0)
                    top[p, :, cols] += first[0:HALF]
                    side[p, 0:half - HALF, :] += first[HALF:half]
                    side[p, half - HALF:TILE - PATCH, :] += second[0:half - HALF]
                    bottom[p, :, cols] += second[half - HALF:half]
    for copy in writes:
        copy.start()
    for copy in writes:
        copy.wait()


def finish(core, ill, total, strips):
    rate = (CAP * lax.axis_size("row") * lax.axis_size("col")) ** (-0.5)
    return pl.pallas_call(
        functools.partial(finish_kernel, rate),
        out_shape=(f32(2, TILE, TILE), f32(2, PATCH, PATCH)),
        in_specs=[ANY, IN_VMEM, IN_VMEM] + [ANY] * 8,
        out_specs=(ANY, IN_VMEM),
        input_output_aliases={0: 0},
        scratch_shapes=[
            pltpu.VMEM((2, HALF, TILE), jnp.float32), pltpu.VMEM((2, HALF, TILE), jnp.float32),
            pltpu.VMEM((2, TILE - PATCH, PATCH), jnp.float32), pltpu.VMEM((2, TILE - PATCH, PATCH), jnp.float32),
            pltpu.SemaphoreType.DMA((4,)), pltpu.SemaphoreType.DMA((8,)),
        ] + [pltpu.VMEM(strip.shape, jnp.float32) for strip in STRIPS],
        compiler_params=pltpu.CompilerParams(vmem_limit_bytes=58 * 2**20),
    )(core, ill, total.reshape(2, PATCH, PATCH), *strips)


def shards(object_field, illumination, positions, slot_counts, amplitudes):
    shared = (jnp.swapaxes(positions, 2, 3), slot_counts, object_field, illumination, amplitudes, jnp.asarray(tables()))
    *halo, terms, hearly = run_early(*shared)
    core, *rest = run_slots(*shared, terms, hearly, halo)
    edges, h = rest[:8], rest[8]
    *strips, total = return_edges(h, edges)
    return finish(core, illumination, total, strips)


def solution(mesh):
    placed = (
        P(None, "row", "col"),
        P(),
        P("row", "col", None, None),
        P("row", "col"),
        P("row", "col", None, None, None),
    )
    return jax.shard_map(
        shards, mesh=mesh, in_specs=placed, out_specs=(P(None, "row", "col"), P()), check_vma=False
    )
```

```python
import functools
import math

import jax
import jax.numpy as jnp
import ml_dtypes
import numpy as np
from jax import lax
from jax.experimental import pallas as pl
from jax.experimental.pallas import tpu as pltpu
from jax.sharding import PartitionSpec as P

MESH = pl.DeviceIdType.MESH
PATCH = 128
HALF = 64
TILE = 1024
CAP = 64
LANE_TILES = TILE // PATCH
GROUP = 16
GROUP_FAR = 8
CHUNKS = 4
PACE = (0, 0, 1, 2, 4)
RING = 8
step_object = 0.25
DIRS = ((1, 0), (-1, 0), (0, 1), (0, -1), (1, 1), (1, -1), (-1, 1), (-1, -1))
SMALL_ROWS = 16
ANY = pl.BlockSpec(memory_space=pltpu.HBM)
IN_VMEM = pl.BlockSpec(memory_space=pltpu.VMEM)
IN_SMEM = pl.BlockSpec(memory_space=pltpu.SMEM)


def f32(*shape):
    return jax.ShapeDtypeStruct(shape, jnp.float32)


STRIPS = (
    f32(2, HALF, TILE), f32(2, HALF, TILE), f32(2, TILE // 2, PATCH), f32(2, TILE // 2, PATCH),
    f32(2, HALF, PATCH), f32(2, HALF, PATCH), f32(2, HALF, PATCH), f32(2, HALF, PATCH),
)


def tables():
    ids = np.arange(PATCH)
    angles = (np.outer(ids, ids) % PATCH) * (2 * math.pi / PATCH)
    cosine, sine = np.cos(angles) / math.sqrt(PATCH), np.sin(angles) / math.sqrt(PATCH)
    forward = np.block([[cosine, -sine], [sine, cosine]])
    out = []
    for matrix in (forward, forward.T):
        high = matrix.astype(np.float32).astype(ml_dtypes.bfloat16)
        out += [high, (matrix - high.astype(np.float64)).astype(np.float32).astype(ml_dtypes.bfloat16)]
    return np.stack(out)


def place():
    return lax.axis_index("row"), lax.axis_index("col"), lax.axis_size("row"), lax.axis_size("col")


def exists(da, db):
    a, b, rows, cols = place()
    return (a + da >= 0) & (a + da < rows) & (b + db >= 0) & (b + db < cols)


def strip_copy(d, src, dst, send_sem, recv_sem):
    a, b, _, _ = place()
    da, db = DIRS[d]
    return pltpu.make_async_remote_copy(
        src_ref=src, dst_ref=dst, send_sem=send_sem.at[d], recv_sem=recv_sem.at[d],
        device_id=(a + da, b + db), device_id_type=MESH,
    )


def start_strips(srcs, dsts, send_sem, recv_sem, which=range(8)):
    for d in which:
        da, db = DIRS[d]

        @pl.when(exists(da, db))
        def _():
            strip_copy(d, srcs[d], dsts[d], send_sem, recv_sem).start()


def wait_strips(srcs, dsts, send_sem, recv_sem, which=range(8)):
    for d in which:
        da, db = DIRS[d]

        @pl.when(exists(-da, -db))
        def _():
            strip_copy(d, srcs[d], dsts[d], send_sem, recv_sem).wait_recv()

        @pl.when(exists(da, db))
        def _():
            strip_copy(d, srcs[d], dsts[d], send_sem, recv_sem).wait_send()


def greet_strips(barrier, dirs):
    a, b, _, _ = place()
    for da, db in dirs:
        @pl.when(exists(da, db))
        def _():
            pl.semaphore_signal(barrier, inc=1, device_id=(a + da, b + db), device_id_type=MESH)


def folded(low_lanes, first, second):
    keep = (lax.broadcasted_iota(jnp.int32, first.shape, 1) < HALF) == low_lanes
    return jnp.where(keep, first, pltpu.roll(second, HALF, 1))


def split(x):
    high = x.astype(jnp.bfloat16)
    return high, (x - high.astype(jnp.float32)).astype(jnp.bfloat16)


def dot(x, y):
    return jnp.dot(x, y, preferred_element_type=jnp.float32)


def right(xs, high, low):
    parts = [split(x) for x in xs]
    both = dot(jnp.concatenate([half for part in parts for half in part], 0), high)
    rest = dot(jnp.concatenate([part[0] for part in parts], 0), low)
    n = xs[0].shape[0]
    return [both[2 * n * k:2 * n * k + n] + both[2 * n * k + n:2 * n * (k + 1)] + rest[n * k:n * (k + 1)] for k in range(len(xs))]


def left(high, low, x):
    xh, xl = split(x)
    return dot(high, xh) + dot(high, xl) + dot(low, xh)


def side_by_side(y):
    return jnp.concatenate([jnp.concatenate([y[:PATCH, c:c + PATCH], y[PATCH:, c:c + PATCH]], 1) for c in (0, PATCH)], 0)


def project(z, a):
    z_r, z_i = z[:PATCH], z[PATCH:]
    factor = a * jnp.minimum(lax.rsqrt(z_r * z_r + z_i * z_i), 2.0)
    return jnp.concatenate([factor * z_r, factor * z_i], 0)


def solve(waves, amps, tab):
    fh, fl, bh, bl = tab[0], tab[1], tab[2], tab[3]
    pairs = range(len(waves) // 2)
    held = [jnp.concatenate([jnp.concatenate(waves[k], 1) for k in (2 * p, 2 * p + 1)], 0) for p in pairs]
    cut = len(pairs) // 2
    for tick in range(5):
        for stage, part in ((tick, list(pairs[:cut])), (tick - 1, list(pairs[cut:]))):
            if stage in (0, 3):
                done = right([held[p] for p in part], *((fh, fl) if stage == 0 else (bh, bl)))
            elif stage == 1:
                done = [project(left(bh, bl, side_by_side(held[p])), amps[p]) for p in part]
            elif stage == 2:
                done = [side_by_side(left(fh, fl, held[p])) for p in part]
            else:
                continue
            for p, value in zip(part, done):
                held[p] = value
    return [(n[r:r + PATCH, :PATCH], n[r:r + PATCH, PATCH:]) for n in held for r in (0, PATCH)]


def patch_wave(buf, ill, rows, ta, tb, shift, first):
    o_r = jnp.where(first, buf[0, ta, rows, :], buf[0, tb, rows, :])
    o_i = jnp.where(first, buf[1, ta, rows, :], buf[1, tb, rows, :])
    p_r, p_i = pltpu.roll(ill[0], shift, 1), pltpu.roll(ill[1], shift, 1)
    return (o_r, o_i, p_r, p_i), (p_r * o_r - p_i * o_i, p_r * o_i + p_i * o_r)


def gradients(parts, wave, new):
    o_r, o_i, p_r, p_i = parts
    c_r, c_i = new[0] - wave[0], new[1] - wave[1]
    terms = (p_r * c_r + p_i * c_i, p_r * c_i - p_i * c_r)
    return terms, (o_r * c_r + o_i * c_i, o_r * c_i - o_i * c_r)


def inside(row, column):
    return (row >= HALF) & (row <= TILE - HALF) & (column >= HALF) & (column <= TILE - HALF)


def early_kernel(pos, cnt, obj, ill, amp, tab, *refs):
    strips, terms, hout = refs[:8], refs[8], refs[9]
    ob, packed, staged, hacc, ampbuf, sem, asem, tsem, send_sem, recv_sem = refs[10:]
    a, b, rows, cols = place()
    count = cnt[0, 0]
    steps = CAP // GROUP
    barrier = pltpu.get_barrier_semaphore()
    greet_strips(barrier, DIRS)
    order = (LANE_TILES - 1, 0) + tuple(range(1, LANE_TILES - 1))
    reads = {
        (p, t): pltpu.make_async_copy(obj.at[p, :, t * PATCH:(t + 1) * PATCH], ob.at[p, t], sem.at[p * LANE_TILES + t])
        for t in order for p in range(2)
    }
    for copy in reads.values():
        copy.start()

    def amp_copy(i):
        return pltpu.make_async_copy(amp.at[0, 0, pl.ds(i * GROUP, GROUP)], ampbuf.at[i], asem.at[i])

    for i in range(steps):
        amp_copy(i).start()
    high = 1 + (a > 0).astype(jnp.int32) + (a < rows - 1).astype(jnp.int32)
    wide = 1 + (b > 0).astype(jnp.int32) + (b < cols - 1).astype(jnp.int32)
    pl.semaphore_wait(barrier, high * wide - 1)
    row_part = {1: slice(TILE - HALF, TILE), -1: slice(0, HALF), 0: slice(0, TILE)}
    col_part = {1: slice(TILE - PATCH, TILE), -1: slice(0, PATCH), 0: slice(0, TILE)}
    srcs = [obj.at[:, row_part[da], col_part[db]] for da, db in DIRS]
    srcs[2], srcs[3] = packed.at[0], packed.at[1]
    start_strips(srcs, strips, send_sem, recv_sem, (0, 1, 4, 5, 6, 7))
    half = TILE // 2
    for n, t in enumerate((LANE_TILES - 1, 0)):
        for p in range(2):
            reads[p, t].wait()
            packed[n, p] = folded(n == 1, ob[p, t, 0:half, :], ob[p, t, half:TILE, :])
        start_strips(srcs, strips, send_sem, recv_sem, (2 + n,))
    for p in range(2):
        ob[p, LANE_TILES] = jnp.zeros((TILE, PATCH), jnp.float32)
    hacc[...] = jnp.zeros_like(hacc)
    for t in order[2:]:
        for p in range(2):
            reads[p, t].wait()
    lane = lax.broadcasted_iota(jnp.int32, (PATCH, PATCH), 1)

    def term_copy(i):
        return pltpu.make_async_copy(staged.at[lax.rem(i, 2)], terms.at[pl.ds(i * GROUP, GROUP)], tsem.at[lax.rem(i, 2)])

    def step(i, carry):
        amp_copy(i).wait()
        info, waves = [], []
        for g in range(GROUP):
            s = i * GROUP + g
            row, column = pos[0, 0, 0, s], pos[0, 0, 1, s]
            good = inside(row, column) & (s < count)
            start = jnp.where(good, row - HALF, 0)
            at = jnp.where(good, column - HALF, 0)
            t, shift = at >> 7, at & (PATCH - 1)
            ta = jnp.where(good, t, LANE_TILES)
            tb = jnp.where(good, jnp.minimum(t + 1, LANE_TILES - 1), LANE_TILES)
            parts, wave = patch_wave(ob, ill, pl.ds(start, PATCH), ta, tb, shift, lane >= shift)
            info.append((parts, shift))
            waves.append(wave)
        amps = [jnp.concatenate([ampbuf[i, g], ampbuf[i, g + 1]], 1) for g in range(0, GROUP, 2)]
        news = solve(waves, amps, tab)

        @pl.when(i >= 2)
        def _():
            term_copy(i - 2).wait()
        for g in range(GROUP):
            parts, shift = info[g]
            out, h = gradients(parts, waves[g], news[g])
            for p in range(2):
                staged[lax.rem(i, 2), g, p] = out[p]
                hacc[p * PATCH:(p + 1) * PATCH] += pltpu.roll(h[p], PATCH - shift, 1)
        term_copy(i).start()
        return carry

    lax.fori_loop(0, steps, step, 0)
    hout[...] = hacc[...]
    for i in (steps - 2, steps - 1):
        term_copy(i).wait()
    wait_strips(srcs, strips, send_sem, recv_sem)


def run_early(positions, slot_counts, obj, ill, amplitudes, tab):
    dma = pltpu.SemaphoreType.DMA
    return pl.pallas_call(
        early_kernel,
        out_shape=STRIPS + (f32(CAP, 2, PATCH, PATCH), f32(2 * PATCH, PATCH)),
        in_specs=[IN_SMEM, IN_SMEM, ANY, IN_VMEM, ANY, IN_VMEM],
        out_specs=(ANY,) * 9 + (IN_VMEM,),
        scratch_shapes=[
            pltpu.VMEM((2, LANE_TILES + 1, TILE, PATCH), jnp.float32), pltpu.VMEM((2, 2, TILE // 2, PATCH), jnp.float32),
            pltpu.VMEM((2, GROUP, 2, PATCH, PATCH), jnp.float32), pltpu.VMEM((2 * PATCH, PATCH), jnp.float32),
            pltpu.VMEM((CAP // GROUP, GROUP, PATCH, PATCH), jnp.float32),
            dma((2 * LANE_TILES,)), dma((CAP // GROUP,)), dma((2,)), dma((8,)), dma((8,)),
        ],
        compiler_params=pltpu.CompilerParams(collective_id=0, has_side_effects=True, vmem_limit_bytes=58 * 2**20),
    )(positions, slot_counts, obj, ill, amplitudes, tab)


def border(d):
    da, db = DIRS[d]
    rows = {1: slice(0, HALF), -1: slice(HALF + TILE, 2 * HALF + TILE), 0: slice(HALF, HALF + TILE)}[da]
    return rows, {1: 0, -1: LANE_TILES + 1, 0: None}[db]


def border_views(buf, strip, d):
    rows, tile = border(d)
    if DIRS[d][0] == 0:
        return [(strip, buf.at[:, tile, HALF:HALF + TILE // 2, :])]
    if tile is not None:
        return [(strip, buf.at[:, tile, rows, :])]
    return [
        (strip.at[p, :, t * PATCH:(t + 1) * PATCH], buf.at[p, t + 1, rows, :])
        for p in range(2) for t in range(LANE_TILES)
    ]


def slots_kernel(pos, cnt, obj, ill, amp, tab, terms, hearly, *refs):
    halo, out, edges, hout = refs[:8], refs[8], refs[9:17], refs[17]
    ob, gr, hacc, ampbuf, held, near, far, sem, asem, tsem, osem = refs[18:]
    count = cnt[0, 0]
    body_copies = [
        pltpu.make_async_copy(obj.at[p, :, t * PATCH:(t + 1) * PATCH], ob.at[p, t + 1, HALF:HALF + TILE, :], sem.at[p * 8 + t])
        for p in range(2) for t in range(LANE_TILES)
    ]

    for copy in body_copies:
        copy.start()

    def listed(s, sizes):
        near[sizes[0]] = s
        far[sizes[1]] = s
        step = inside(pos[0, 0, 0, s], pos[0, 0, 1, s]).astype(jnp.int32)
        return sizes[0] + step, sizes[1] + 1 - step

    n_near, n_far = lax.fori_loop(0, count, listed, (jnp.int32(0), jnp.int32(0)))

    def term_copy(j):
        return pltpu.make_async_copy(terms.at[near[j]], held.at[lax.rem(j, RING)], tsem.at[lax.rem(j, RING)])

    def amp_copy(j):
        return pltpu.make_async_copy(amp.at[0, 0, far[j]], ampbuf.at[j], asem.at[j])

    @pl.loop(0, jnp.minimum(n_near, RING))
    def _(j):
        term_copy(j).start()

    @pl.loop(0, n_far)
    def _(j):
        amp_copy(j).start()

    halo_copies = []
    for d in range(8):
        views = border_views(ob, halo[d], d)
        halo_copies.append([pltpu.make_async_copy(src, dst, osem.at[d, n]) for n, (src, dst) in enumerate(views)])
    for d, (da, db) in enumerate(DIRS):
        @pl.when(exists(-da, -db))
        def _():
            for copy in halo_copies[d]:
                copy.start()

        @pl.when(jnp.logical_not(exists(-da, -db)))
        def _():
            rows, tile = border(d)
            for p in range(2):
                for t in range(1, LANE_TILES + 1) if tile is None else (tile,):
                    ob[p, t, rows, :] = jnp.zeros((rows.stop - rows.start, PATCH), jnp.float32)

    zero = jnp.zeros((PATCH, PATCH), jnp.float32)

    @pl.loop(0, (TILE + PATCH) // PATCH)
    def _(i):
        rows = pl.ds(pl.multiple_of(i * PATCH, PATCH), PATCH)
        for p in range(2):
            for t in range(LANE_TILES + 2):
                gr[p, t, rows, :] = zero
            ob[p, LANE_TILES + 2, rows, :] = zero
    hacc[...] = hearly[...]
    lane = lax.broadcasted_iota(jnp.int32, (PATCH, PATCH), 1)

    def add(rows, t, first, term):
        for p in range(2):
            now = jnp.where(first, gr[p, t, rows, :], gr[p, t + 1, rows, :]) + term[p]
            pltpu.store(gr.at[p, t, rows, :], now, mask=first)
            pltpu.store(gr.at[p, t + 1, rows, :], now, mask=jnp.logical_not(first))

    @pl.loop(0, n_near)
    def _(j):
        s = near[j]
        term_copy(j).wait()
        column = pos[0, 0, 1, s] + HALF
        add(pl.ds(pos[0, 0, 0, s], PATCH), column >> 7, lane >= (column & (PATCH - 1)), [held[lax.rem(j, RING), p] for p in range(2)])

        @pl.when(j + RING < n_near)
        def _():
            term_copy(j + RING).start()

    for copy in body_copies:
        copy.wait()
    for d, (da, db) in enumerate(DIRS):
        @pl.when(exists(-da, -db))
        def _():
            for copy in halo_copies[d]:
                copy.wait()
            if da == 0:
                tile = border(d)[1]
                for p in range(2):
                    ob[p, tile, HALF + TILE // 2:HALF + TILE, :] = pltpu.roll(ob[p, tile, HALF:HALF + TILE // 2, :], HALF, 1)

    @pl.loop(0, n_far)
    def _(j):
        amp_copy(j).wait()

    def step(i, carry):
        info, waves, slots = [], [], []
        for g in range(GROUP_FAR):
            live = i * GROUP_FAR + g < n_far
            j = jnp.where(live, i * GROUP_FAR + g, 0)
            s = far[j]
            rows = pl.ds(pos[0, 0, 0, s], PATCH)
            column = pos[0, 0, 1, s] + HALF
            t, shift = column >> 7, column & (PATCH - 1)
            first = lane >= shift
            ta, tb = jnp.where(live, t, LANE_TILES + 2), jnp.where(live, t + 1, LANE_TILES + 2)
            parts, wave = patch_wave(ob, ill, rows, ta, tb, shift, first)
            info.append((rows, t, shift, first, parts))
            waves.append(wave)
            slots.append(j)
        amps = [jnp.concatenate([ampbuf[slots[g]], ampbuf[slots[g + 1]]], 1) for g in range(0, GROUP_FAR, 2)]
        news = solve(waves, amps, tab)
        for g in range(GROUP_FAR):
            rows, t, shift, first, parts = info[g]
            term, h = gradients(parts, waves[g], news[g])
            add(rows, t, first, term)
            for p in range(2):
                hacc[p * PATCH:(p + 1) * PATCH] += pltpu.roll(h[p], PATCH - shift, 1)
        return carry

    lax.fori_loop(0, (n_far + GROUP_FAR - 1) // GROUP_FAR, step, 0)
    hout[...] = hacc[...]
    last = []
    for tile in (0, LANE_TILES + 1):
        for p in range(2):
            gr[p, tile, HALF:HALF + TILE // 2, :] = folded(
                tile > 0, gr[p, tile, HALF:HALF + TILE // 2, :], gr[p, tile, HALF + TILE // 2:HALF + TILE, :])
    for d in range(8):
        da, db = DIRS[d]
        views = border_views(gr, edges[d], DIRS.index((-da, -db)))
        last += [pltpu.make_async_copy(dst, src, osem.at[d, n]) for n, (src, dst) in enumerate(views)]
    for copy in last:
        copy.start()
    for p in range(2):
        for t in range(LANE_TILES):
            @pl.loop(0, TILE // PATCH)
            def _(i):
                rows = pl.ds(pl.multiple_of(HALF + i * PATCH, HALF), PATCH)
                ob[p, t + 1, rows, :] += step_object * gr[p, t + 1, rows, :]
            copy = pltpu.make_async_copy(
                ob.at[p, t + 1, HALF:HALF + TILE, :], out.at[p, :, t * PATCH:(t + 1) * PATCH], sem.at[p * 8 + t])
            copy.start()
            last.append(copy)
    for copy in last:
        copy.wait()


def run_slots(positions, slot_counts, obj, ill, amplitudes, tab, terms, hearly, halo):
    dma = pltpu.SemaphoreType.DMA
    return pl.pallas_call(
        slots_kernel,
        out_shape=(f32(2, TILE, TILE),) + STRIPS + (f32(2 * PATCH, PATCH),),
        in_specs=[IN_SMEM, IN_SMEM, ANY, IN_VMEM, ANY, IN_VMEM, ANY, IN_VMEM] + [ANY] * 8,
        out_specs=(ANY,) * 9 + (IN_VMEM,),
        scratch_shapes=[
            pltpu.VMEM((2, LANE_TILES + 3, TILE + PATCH, PATCH), jnp.float32),
            pltpu.VMEM((2, LANE_TILES + 2, TILE + PATCH, PATCH), jnp.float32),
            pltpu.VMEM((2 * PATCH, PATCH), jnp.float32), pltpu.VMEM((CAP, PATCH, PATCH), jnp.float32),
            pltpu.VMEM((RING, 2, PATCH, PATCH), jnp.float32), pltpu.SMEM((CAP,), jnp.int32), pltpu.SMEM((CAP,), jnp.int32),
            dma((16,)), dma((CAP,)), dma((RING,)), dma((8, 16)),
        ],
        compiler_params=pltpu.CompilerParams(vmem_limit_bytes=58 * 2**20),
    )(positions, slot_counts, obj, ill, amplitudes, tab, terms, hearly, *halo)


def return_kernel(h, *refs):
    edges, strips, total = refs[:8], refs[8:16], refs[16]
    other, mine, pieces, sums, gathered, send_sem, recv_sem, s0, r0, s1, r1, s2, r2, s3, r3 = refs[17:]
    a, b, rows, cols = place()
    chips = cols // 2
    q, core = b // 2, lax.rem(b, 2)
    partner = (a, b + 1 - 2 * core)

    def row_peer(k):
        return lax.rem(a + k, rows)

    def chip_peer(k):
        return lax.rem(q + k, chips)

    barrier = pltpu.get_barrier_semaphore()
    greet_strips(barrier, DIRS[4:])
    pl.semaphore_signal(barrier, inc=1, device_id=partner, device_id_type=MESH)
    for k in range(1, rows):
        pl.semaphore_signal(barrier, inc=1, device_id=(row_peer(k), b), device_id_type=MESH)
    for k in range(1, chips):
        pl.semaphore_signal(barrier, inc=1, device_id=(a, chip_peer(k) * 2 + core), device_id_type=MESH)
    across = ((core == 1) & (b < cols - 1)) | ((core == 0) & (b > 0))
    side = b + 2 * core - 1

    @pl.when(across)
    def _():
        pl.semaphore_signal(barrier, inc=1, device_id=(a, side), device_id_type=MESH)
    high = (a > 0).astype(jnp.int32) + (a < rows - 1).astype(jnp.int32)
    wide = (b > 0).astype(jnp.int32) + (b < cols - 1).astype(jnp.int32)
    pl.semaphore_wait(barrier, 1 + rows - 1 + chips - 1 + across.astype(jnp.int32) + high * wide)

    def piece_rows(k):
        return pl.ds(pl.multiple_of(k * SMALL_ROWS, SMALL_ROWS), SMALL_ROWS)

    def half_rows(k):
        return pl.ds(pl.multiple_of(k * PATCH, PATCH), PATCH)

    def remote(src, dst, send, recv, device):
        return pltpu.make_async_remote_copy(
            src_ref=src, dst_ref=dst, send_sem=send, recv_sem=recv, device_id=device, device_id_type=MESH)

    def swap():
        return remote(h.at[half_rows(1 - core)], other, s0.at[0], r0.at[0], partner)

    def scatter(peer, slot):
        return remote(mine.at[piece_rows(peer)], pieces.at[slot], s1.at[peer], r1.at[slot], (peer, b))

    def share(peer, slot):
        return remote(sums.at[slot], sums.at[slot], s2.at[peer], r2.at[slot], (a, peer * 2 + core))

    def gather(peer, slot):
        return remote(gathered.at[core, slot], gathered.at[core, slot], s3.at[peer], r3.at[slot], (peer, b))

    def hand(which):
        return remote(gathered.at[which], gathered.at[which], s0.at[1], r0.at[1], partner)

    def parts(refs, c):
        return [
            ref if d >= 4 else ref.at[:, c * (HALF // CHUNKS):(c + 1) * (HALF // CHUNKS), :] if d < 2
            else ref.at[:, c * (TILE // 2 // CHUNKS):(c + 1) * (TILE // 2 // CHUNKS), :]
            for d, ref in enumerate(refs)
        ]

    def send_strips(stage):
        for c in range(PACE[stage], PACE[stage + 1]):
            start_strips(parts(edges, c), parts(strips, c), send_sem.at[c], recv_sem.at[c], range(8) if c == 0 else range(4))

    swap().start()
    send_strips(0)
    swap().wait_recv()
    mine[...] = h[half_rows(core), :] + other[...]
    for k in range(1, rows):
        scatter(row_peer(k), a).start()
    send_strips(1)
    pieces[a] = mine[piece_rows(a), :]
    for k in range(1, rows):
        scatter(a, row_peer(k)).wait_recv()
    sums[q] = jnp.sum(pieces[...], axis=0)
    for k in range(1, chips):
        share(chip_peer(k), q).start()
    send_strips(2)
    for k in range(1, chips):
        share(q, chip_peer(k)).wait_recv()
    gathered[core, a] = jnp.sum(sums[...], axis=0)
    for k in range(1, rows):
        gather(row_peer(k), a).start()
    send_strips(3)
    for k in range(1, rows):
        gather(a, row_peer(k)).wait_recv()
    hand(core).start()
    hand(1 - core).wait_recv()
    total[...] = gathered[...]
    swap().wait_send()
    hand(core).wait_send()
    for k in range(1, rows):
        scatter(row_peer(k), a).wait_send()
        gather(row_peer(k), a).wait_send()
    for k in range(1, chips):
        share(chip_peer(k), q).wait_send()
    for c in range(CHUNKS):
        wait_strips(parts(edges, c), parts(strips, c), send_sem.at[c], recv_sem.at[c], range(8) if c == 0 else range(4))


def return_edges(h, edges):
    rows, chips = lax.axis_size("row"), lax.axis_size("col") // 2
    dma = pltpu.SemaphoreType.DMA
    return pl.pallas_call(
        return_kernel,
        out_shape=STRIPS + (f32(2, rows, SMALL_ROWS, PATCH),),
        in_specs=[IN_VMEM] + [ANY] * 8,
        out_specs=(ANY,) * 8 + (IN_VMEM,),
        scratch_shapes=[
            pltpu.VMEM((PATCH, PATCH), jnp.float32), pltpu.VMEM((PATCH, PATCH), jnp.float32),
            pltpu.VMEM((rows, SMALL_ROWS, PATCH), jnp.float32), pltpu.VMEM((chips, SMALL_ROWS, PATCH), jnp.float32),
            pltpu.VMEM((2, rows, SMALL_ROWS, PATCH), jnp.float32), dma((CHUNKS, 8)), dma((CHUNKS, 8)),
            dma((2,)), dma((2,)), dma((rows,)), dma((rows,)), dma((chips,)), dma((chips,)), dma((rows,)), dma((rows,)),
        ],
        compiler_params=pltpu.CompilerParams(collective_id=1, has_side_effects=True, vmem_limit_bytes=58 * 2**20),
    )(h, *edges)


def finish_kernel(rate, core, ill, total, *refs):
    strips, out, probe = refs[:8], refs[8], refs[9]
    top, bottom, west, east, sem, strip_sem = refs[10:16]
    held = refs[16:]
    middle = slice(HALF, TILE - HALF)
    parts = (
        (top, out.at[:, 0:HALF, :]), (bottom, out.at[:, TILE - HALF:TILE, :]),
        (west, out.at[:, middle, 0:PATCH]), (east, out.at[:, middle, TILE - PATCH:TILE]),
    )
    reads = [pltpu.make_async_copy(hbm, vmem, sem.at[n]) for n, (vmem, hbm) in enumerate(parts)]
    writes = [pltpu.make_async_copy(vmem, hbm, sem.at[n]) for n, (vmem, hbm) in enumerate(parts)]
    fetches = [pltpu.make_async_copy(strips[d], held[d], strip_sem.at[d]) for d in range(8)]
    for d, (da, db) in enumerate(DIRS):
        @pl.when(exists(-da, -db))
        def _():
            fetches[d].start()
    for copy in reads:
        copy.start()
    probe[...] = ill[...] + rate * total[...]
    half = TILE // 2

    def add(d):
        da, db = DIRS[d]

        @pl.when(exists(-da, -db))
        def _():
            fetches[d].wait()
            if da != 0:
                target = top if da > 0 else bottom
                cols = {0: slice(0, TILE), 1: slice(0, PATCH), -1: slice(TILE - PATCH, TILE)}[db]
                target[:, :, cols] += step_object * held[d][...]
            else:
                side = west if db > 0 else east
                cols = slice(0, PATCH) if db > 0 else slice(TILE - PATCH, TILE)
                low = lax.broadcasted_iota(jnp.int32, (half, PATCH), 1) < HALF
                keep = low if db > 0 else jnp.logical_not(low)
                for p in range(2):
                    first = jnp.where(keep, step_object * held[d][p], 0.0)
                    second = jnp.where(keep, pltpu.roll(step_object * held[d][p], HALF, 1), 0.0)
                    top[p, :, cols] += first[0:HALF]
                    side[p, 0:half - HALF, :] += first[HALF:half]
                    side[p, half - HALF:TILE - PATCH, :] += second[0:half - HALF]
                    bottom[p, :, cols] += second[half - HALF:half]

    for n in (0, 1, 2):
        reads[n].wait()
    add(2)
    writes[2].start()
    reads[3].wait()
    add(3)
    writes[3].start()
    for d in (0, 4, 5):
        add(d)
    writes[0].start()
    for d in (1, 6, 7):
        add(d)
    writes[1].start()
    for copy in writes:
        copy.wait()


def finish(core, ill, total, strips):
    rate = (CAP * lax.axis_size("row") * lax.axis_size("col")) ** (-0.5)
    return pl.pallas_call(
        functools.partial(finish_kernel, rate),
        out_shape=(f32(2, TILE, TILE), f32(2, PATCH, PATCH)),
        in_specs=[ANY, IN_VMEM, IN_VMEM] + [ANY] * 8,
        out_specs=(ANY, IN_VMEM),
        input_output_aliases={0: 0},
        scratch_shapes=[
            pltpu.VMEM((2, HALF, TILE), jnp.float32), pltpu.VMEM((2, HALF, TILE), jnp.float32),
            pltpu.VMEM((2, TILE - PATCH, PATCH), jnp.float32), pltpu.VMEM((2, TILE - PATCH, PATCH), jnp.float32),
            pltpu.SemaphoreType.DMA((4,)), pltpu.SemaphoreType.DMA((8,)),
        ] + [pltpu.VMEM(strip.shape, jnp.float32) for strip in STRIPS],
        compiler_params=pltpu.CompilerParams(vmem_limit_bytes=58 * 2**20),
    )(core, ill, total.reshape(2, PATCH, PATCH), *strips)


def shards(object_field, illumination, positions, slot_counts, amplitudes):
    shared = (jnp.swapaxes(positions, 2, 3), slot_counts, object_field, illumination, amplitudes, jnp.asarray(tables()))
    *halo, terms, hearly = run_early(*shared)
    core, *rest = run_slots(*shared, terms, hearly, halo)
    edges, h = rest[:8], rest[8]
    *strips, total = return_edges(h, edges)
    return finish(core, illumination, total, strips)


def solution(mesh):
    placed = (
        P(None, "row", "col"),
        P(),
        P("row", "col", None, None),
        P("row", "col"),
        P("row", "col", None, None, None),
    )
    return jax.shard_map(
        shards, mesh=mesh, in_specs=placed, out_specs=(P(None, "row", "col"), P()), check_vma=False
    )
```

```python
import functools
import math

import jax
import jax.numpy as jnp
import ml_dtypes
import numpy as np
from jax import lax
from jax.experimental import pallas as pl
from jax.experimental.pallas import tpu as pltpu
from jax.sharding import PartitionSpec as P

MESH = pl.DeviceIdType.MESH
PATCH = 128
HALF = 64
TILE = 1024
CAP = 64
LANE_TILES = TILE // PATCH
GROUP = 16
GROUP_FAR = 8
CHUNKS = 4
PACE = (0, 1, 2, 3, 4)
RING = 8
step_object = 0.25
DIRS = ((1, 0), (-1, 0), (0, 1), (0, -1), (1, 1), (1, -1), (-1, 1), (-1, -1))
SMALL_ROWS = 16
ANY = pl.BlockSpec(memory_space=pltpu.HBM)
IN_VMEM = pl.BlockSpec(memory_space=pltpu.VMEM)
IN_SMEM = pl.BlockSpec(memory_space=pltpu.SMEM)


def f32(*shape):
    return jax.ShapeDtypeStruct(shape, jnp.float32)


STRIPS = (
    f32(2, HALF, TILE), f32(2, HALF, TILE), f32(2, TILE // 2, PATCH), f32(2, TILE // 2, PATCH),
    f32(2, HALF, PATCH), f32(2, HALF, PATCH), f32(2, HALF, PATCH), f32(2, HALF, PATCH),
)


def tables():
    ids = np.arange(PATCH)
    angles = (np.outer(ids, ids) % PATCH) * (2 * math.pi / PATCH)
    cosine, sine = np.cos(angles) / math.sqrt(PATCH), np.sin(angles) / math.sqrt(PATCH)
    forward = np.block([[cosine, -sine], [sine, cosine]])
    out = []
    for matrix in (forward, forward.T):
        high = matrix.astype(np.float32).astype(ml_dtypes.bfloat16)
        out += [high, (matrix - high.astype(np.float64)).astype(np.float32).astype(ml_dtypes.bfloat16)]
    return np.stack(out)


def place():
    return lax.axis_index("row"), lax.axis_index("col"), lax.axis_size("row"), lax.axis_size("col")


def exists(da, db):
    a, b, rows, cols = place()
    return (a + da >= 0) & (a + da < rows) & (b + db >= 0) & (b + db < cols)


def strip_copy(d, src, dst, send_sem, recv_sem):
    a, b, _, _ = place()
    da, db = DIRS[d]
    return pltpu.make_async_remote_copy(
        src_ref=src, dst_ref=dst, send_sem=send_sem.at[d], recv_sem=recv_sem.at[d],
        device_id=(a + da, b + db), device_id_type=MESH,
    )


def start_strips(srcs, dsts, send_sem, recv_sem, which=range(8)):
    for d in which:
        da, db = DIRS[d]

        @pl.when(exists(da, db))
        def _():
            strip_copy(d, srcs[d], dsts[d], send_sem, recv_sem).start()


def wait_strips(srcs, dsts, send_sem, recv_sem, which=range(8)):
    for d in which:
        da, db = DIRS[d]

        @pl.when(exists(-da, -db))
        def _():
            strip_copy(d, srcs[d], dsts[d], send_sem, recv_sem).wait_recv()

        @pl.when(exists(da, db))
        def _():
            strip_copy(d, srcs[d], dsts[d], send_sem, recv_sem).wait_send()


def greet_strips(barrier, dirs):
    a, b, _, _ = place()
    for da, db in dirs:
        @pl.when(exists(da, db))
        def _():
            pl.semaphore_signal(barrier, inc=1, device_id=(a + da, b + db), device_id_type=MESH)


def folded(low_lanes, first, second):
    keep = (lax.broadcasted_iota(jnp.int32, first.shape, 1) < HALF) == low_lanes
    return jnp.where(keep, first, pltpu.roll(second, HALF, 1))


def split(x):
    high = x.astype(jnp.bfloat16)
    return high, (x - high.astype(jnp.float32)).astype(jnp.bfloat16)


def dot(x, y):
    return jnp.dot(x, y, preferred_element_type=jnp.float32)


def right(xs, high, low):
    parts = [split(x) for x in xs]
    both = dot(jnp.concatenate([half for part in parts for half in part], 0), high)
    rest = dot(jnp.concatenate([part[0] for part in parts], 0), low)
    n = xs[0].shape[0]
    return [both[2 * n * k:2 * n * k + n] + both[2 * n * k + n:2 * n * (k + 1)] + rest[n * k:n * (k + 1)] for k in range(len(xs))]


def left(high, low, x):
    xh, xl = split(x)
    return dot(high, xh) + dot(high, xl) + dot(low, xh)


def side_by_side(y):
    return jnp.concatenate([jnp.concatenate([y[:PATCH, c:c + PATCH], y[PATCH:, c:c + PATCH]], 1) for c in (0, PATCH)], 0)


def project(z, a):
    z_r, z_i = z[:PATCH], z[PATCH:]
    factor = a * jnp.minimum(lax.rsqrt(z_r * z_r + z_i * z_i), 2.0)
    return jnp.concatenate([factor * z_r, factor * z_i], 0)


def solve(waves, amps, tab):
    fh, fl, bh, bl = tab[0], tab[1], tab[2], tab[3]
    pairs = range(len(waves) // 2)
    held = [jnp.concatenate([jnp.concatenate(waves[k], 1) for k in (2 * p, 2 * p + 1)], 0) for p in pairs]
    cut = len(pairs) // 2
    for tick in range(5):
        for stage, part in ((tick, list(pairs[:cut])), (tick - 1, list(pairs[cut:]))):
            if stage in (0, 3):
                done = right([held[p] for p in part], *((fh, fl) if stage == 0 else (bh, bl)))
            elif stage == 1:
                done = [project(left(bh, bl, side_by_side(held[p])), amps[p]) for p in part]
            elif stage == 2:
                done = [side_by_side(left(fh, fl, held[p])) for p in part]
            else:
                continue
            for p, value in zip(part, done):
                held[p] = value
    return [(n[r:r + PATCH, :PATCH], n[r:r + PATCH, PATCH:]) for n in held for r in (0, PATCH)]


def patch_wave(buf, ill, rows, ta, tb, shift, first):
    o_r = jnp.where(first, buf[0, ta, rows, :], buf[0, tb, rows, :])
    o_i = jnp.where(first, buf[1, ta, rows, :], buf[1, tb, rows, :])
    p_r, p_i = pltpu.roll(ill[0], shift, 1), pltpu.roll(ill[1], shift, 1)
    return (o_r, o_i, p_r, p_i), (p_r * o_r - p_i * o_i, p_r * o_i + p_i * o_r)


def gradients(parts, wave, new):
    o_r, o_i, p_r, p_i = parts
    c_r, c_i = new[0] - wave[0], new[1] - wave[1]
    terms = (p_r * c_r + p_i * c_i, p_r * c_i - p_i * c_r)
    return terms, (o_r * c_r + o_i * c_i, o_r * c_i - o_i * c_r)


def inside(row, column):
    return (row >= HALF) & (row <= TILE - HALF) & (column >= HALF) & (column <= TILE - HALF)


def early_kernel(pos, cnt, obj, ill, amp, tab, *refs):
    strips, terms, hout = refs[:8], refs[8], refs[9]
    ob, packed, staged, hacc, ampbuf, sem, asem, tsem, send_sem, recv_sem = refs[10:]
    a, b, rows, cols = place()
    count = cnt[0, 0]
    steps = CAP // GROUP
    barrier = pltpu.get_barrier_semaphore()
    greet_strips(barrier, DIRS)
    order = (LANE_TILES - 1, 0) + tuple(range(1, LANE_TILES - 1))
    reads = {
        (p, t): pltpu.make_async_copy(obj.at[p, :, t * PATCH:(t + 1) * PATCH], ob.at[p, t], sem.at[p * LANE_TILES + t])
        for t in order for p in range(2)
    }
    for copy in reads.values():
        copy.start()

    def amp_copy(i):
        return pltpu.make_async_copy(amp.at[0, 0, pl.ds(i * GROUP, GROUP)], ampbuf.at[i], asem.at[i])

    for i in range(steps):
        amp_copy(i).start()
    high = 1 + (a > 0).astype(jnp.int32) + (a < rows - 1).astype(jnp.int32)
    wide = 1 + (b > 0).astype(jnp.int32) + (b < cols - 1).astype(jnp.int32)
    pl.semaphore_wait(barrier, high * wide - 1)
    row_part = {1: slice(TILE - HALF, TILE), -1: slice(0, HALF), 0: slice(0, TILE)}
    col_part = {1: slice(TILE - PATCH, TILE), -1: slice(0, PATCH), 0: slice(0, TILE)}
    srcs = [obj.at[:, row_part[da], col_part[db]] for da, db in DIRS]
    srcs[2], srcs[3] = packed.at[0], packed.at[1]
    start_strips(srcs, strips, send_sem, recv_sem, (0, 1, 4, 5, 6, 7))
    half = TILE // 2
    for n, t in enumerate((LANE_TILES - 1, 0)):
        for p in range(2):
            reads[p, t].wait()
            packed[n, p] = folded(n == 1, ob[p, t, 0:half, :], ob[p, t, half:TILE, :])
        start_strips(srcs, strips, send_sem, recv_sem, (2 + n,))
    for p in range(2):
        ob[p, LANE_TILES] = jnp.zeros((TILE, PATCH), jnp.float32)
    hacc[...] = jnp.zeros_like(hacc)
    for t in order[2:]:
        for p in range(2):
            reads[p, t].wait()
    lane = lax.broadcasted_iota(jnp.int32, (PATCH, PATCH), 1)

    def term_copy(i):
        return pltpu.make_async_copy(staged.at[lax.rem(i, 2)], terms.at[pl.ds(i * GROUP, GROUP)], tsem.at[lax.rem(i, 2)])

    def step(i, carry):
        amp_copy(i).wait()
        info, waves = [], []
        for g in range(GROUP):
            s = i * GROUP + g
            row, column = pos[0, 0, 0, s], pos[0, 0, 1, s]
            good = inside(row, column) & (s < count)
            start = jnp.where(good, row - HALF, 0)
            at = jnp.where(good, column - HALF, 0)
            t, shift = at >> 7, at & (PATCH - 1)
            ta = jnp.where(good, t, LANE_TILES)
            tb = jnp.where(good, jnp.minimum(t + 1, LANE_TILES - 1), LANE_TILES)
            parts, wave = patch_wave(ob, ill, pl.ds(start, PATCH), ta, tb, shift, lane >= shift)
            info.append((parts, shift))
            waves.append(wave)
        amps = [jnp.concatenate([ampbuf[i, g], ampbuf[i, g + 1]], 1) for g in range(0, GROUP, 2)]
        news = solve(waves, amps, tab)

        @pl.when(i >= 2)
        def _():
            term_copy(i - 2).wait()
        for g in range(GROUP):
            parts, shift = info[g]
            out, h = gradients(parts, waves[g], news[g])
            for p in range(2):
                staged[lax.rem(i, 2), g, p] = out[p]
                hacc[p * PATCH:(p + 1) * PATCH] += pltpu.roll(h[p], PATCH - shift, 1)
        term_copy(i).start()
        return carry

    lax.fori_loop(0, steps, step, 0)
    hout[...] = hacc[...]
    for i in (steps - 2, steps - 1):
        term_copy(i).wait()
    wait_strips(srcs, strips, send_sem, recv_sem)


def run_early(positions, slot_counts, obj, ill, amplitudes, tab):
    dma = pltpu.SemaphoreType.DMA
    return pl.pallas_call(
        early_kernel,
        out_shape=STRIPS + (f32(CAP, 2, PATCH, PATCH), f32(2 * PATCH, PATCH)),
        in_specs=[IN_SMEM, IN_SMEM, ANY, IN_VMEM, ANY, IN_VMEM],
        out_specs=(ANY,) * 9 + (IN_VMEM,),
        scratch_shapes=[
            pltpu.VMEM((2, LANE_TILES + 1, TILE, PATCH), jnp.float32), pltpu.VMEM((2, 2, TILE // 2, PATCH), jnp.float32),
            pltpu.VMEM((2, GROUP, 2, PATCH, PATCH), jnp.float32), pltpu.VMEM((2 * PATCH, PATCH), jnp.float32),
            pltpu.VMEM((CAP // GROUP, GROUP, PATCH, PATCH), jnp.float32),
            dma((2 * LANE_TILES,)), dma((CAP // GROUP,)), dma((2,)), dma((8,)), dma((8,)),
        ],
        compiler_params=pltpu.CompilerParams(collective_id=0, has_side_effects=True, vmem_limit_bytes=58 * 2**20),
    )(positions, slot_counts, obj, ill, amplitudes, tab)


def border(d):
    da, db = DIRS[d]
    rows = {1: slice(0, HALF), -1: slice(HALF + TILE, 2 * HALF + TILE), 0: slice(HALF, HALF + TILE)}[da]
    return rows, {1: 0, -1: LANE_TILES + 1, 0: None}[db]


def border_views(buf, strip, d):
    rows, tile = border(d)
    if DIRS[d][0] == 0:
        return [(strip, buf.at[:, tile, HALF:HALF + TILE // 2, :])]
    if tile is not None:
        return [(strip, buf.at[:, tile, rows, :])]
    return [
        (strip.at[p, :, t * PATCH:(t + 1) * PATCH], buf.at[p, t + 1, rows, :])
        for p in range(2) for t in range(LANE_TILES)
    ]


def slots_kernel(pos, cnt, obj, ill, amp, tab, terms, hearly, *refs):
    halo, out, edges, hout = refs[:8], refs[8], refs[9:17], refs[17]
    ob, gr, hacc, ampbuf, held, near, far, sem, asem, tsem, osem = refs[18:]
    count = cnt[0, 0]
    body_copies = [
        pltpu.make_async_copy(obj.at[p, :, t * PATCH:(t + 1) * PATCH], ob.at[p, t + 1, HALF:HALF + TILE, :], sem.at[p * 8 + t])
        for p in range(2) for t in range(LANE_TILES)
    ]

    for copy in body_copies:
        copy.start()

    def listed(s, sizes):
        near[sizes[0]] = s
        far[sizes[1]] = s
        step = inside(pos[0, 0, 0, s], pos[0, 0, 1, s]).astype(jnp.int32)
        return sizes[0] + step, sizes[1] + 1 - step

    n_near, n_far = lax.fori_loop(0, count, listed, (jnp.int32(0), jnp.int32(0)))

    def term_copy(j):
        return pltpu.make_async_copy(terms.at[near[j]], held.at[lax.rem(j, RING)], tsem.at[lax.rem(j, RING)])

    def amp_copy(j):
        return pltpu.make_async_copy(amp.at[0, 0, far[j]], ampbuf.at[j], asem.at[j])

    @pl.loop(0, jnp.minimum(n_near, RING))
    def _(j):
        term_copy(j).start()

    @pl.loop(0, n_far)
    def _(j):
        amp_copy(j).start()

    halo_copies = []
    for d in range(8):
        views = border_views(ob, halo[d], d)
        halo_copies.append([pltpu.make_async_copy(src, dst, osem.at[d, n]) for n, (src, dst) in enumerate(views)])
    for d, (da, db) in enumerate(DIRS):
        @pl.when(exists(-da, -db))
        def _():
            for copy in halo_copies[d]:
                copy.start()

        @pl.when(jnp.logical_not(exists(-da, -db)))
        def _():
            rows, tile = border(d)
            for p in range(2):
                for t in range(1, LANE_TILES + 1) if tile is None else (tile,):
                    ob[p, t, rows, :] = jnp.zeros((rows.stop - rows.start, PATCH), jnp.float32)

    zero = jnp.zeros((PATCH, PATCH), jnp.float32)

    @pl.loop(0, (TILE + PATCH) // PATCH)
    def _(i):
        rows = pl.ds(pl.multiple_of(i * PATCH, PATCH), PATCH)
        for p in range(2):
            for t in range(LANE_TILES + 2):
                gr[p, t, rows, :] = zero
            ob[p, LANE_TILES + 2, rows, :] = zero
    hacc[...] = hearly[...]
    lane = lax.broadcasted_iota(jnp.int32, (PATCH, PATCH), 1)

    def add(rows, t, first, term):
        for p in range(2):
            now = jnp.where(first, gr[p, t, rows, :], gr[p, t + 1, rows, :]) + term[p]
            pltpu.store(gr.at[p, t, rows, :], now, mask=first)
            pltpu.store(gr.at[p, t + 1, rows, :], now, mask=jnp.logical_not(first))

    @pl.loop(0, n_near)
    def _(j):
        s = near[j]
        term_copy(j).wait()
        column = pos[0, 0, 1, s] + HALF
        add(pl.ds(pos[0, 0, 0, s], PATCH), column >> 7, lane >= (column & (PATCH - 1)), [held[lax.rem(j, RING), p] for p in range(2)])

        @pl.when(j + RING < n_near)
        def _():
            term_copy(j + RING).start()

    for copy in body_copies:
        copy.wait()
    for d, (da, db) in enumerate(DIRS):
        @pl.when(exists(-da, -db))
        def _():
            for copy in halo_copies[d]:
                copy.wait()
            if da == 0:
                tile = border(d)[1]
                for p in range(2):
                    ob[p, tile, HALF + TILE // 2:HALF + TILE, :] = pltpu.roll(ob[p, tile, HALF:HALF + TILE // 2, :], HALF, 1)

    @pl.loop(0, n_far)
    def _(j):
        amp_copy(j).wait()

    def step(i, carry):
        info, waves, slots = [], [], []
        for g in range(GROUP_FAR):
            live = i * GROUP_FAR + g < n_far
            j = jnp.where(live, i * GROUP_FAR + g, 0)
            s = far[j]
            rows = pl.ds(pos[0, 0, 0, s], PATCH)
            column = pos[0, 0, 1, s] + HALF
            t, shift = column >> 7, column & (PATCH - 1)
            first = lane >= shift
            ta, tb = jnp.where(live, t, LANE_TILES + 2), jnp.where(live, t + 1, LANE_TILES + 2)
            parts, wave = patch_wave(ob, ill, rows, ta, tb, shift, first)
            info.append((rows, t, shift, first, parts))
            waves.append(wave)
            slots.append(j)
        amps = [jnp.concatenate([ampbuf[slots[g]], ampbuf[slots[g + 1]]], 1) for g in range(0, GROUP_FAR, 2)]
        news = solve(waves, amps, tab)
        for g in range(GROUP_FAR):
            rows, t, shift, first, parts = info[g]
            term, h = gradients(parts, waves[g], news[g])
            add(rows, t, first, term)
            for p in range(2):
                hacc[p * PATCH:(p + 1) * PATCH] += pltpu.roll(h[p], PATCH - shift, 1)
        return carry

    lax.fori_loop(0, (n_far + GROUP_FAR - 1) // GROUP_FAR, step, 0)
    hout[...] = hacc[...]
    last = []
    for tile in (0, LANE_TILES + 1):
        for p in range(2):
            gr[p, tile, HALF:HALF + TILE // 2, :] = folded(
                tile > 0, gr[p, tile, HALF:HALF + TILE // 2, :], gr[p, tile, HALF + TILE // 2:HALF + TILE, :])
    for d in range(8):
        da, db = DIRS[d]
        views = border_views(gr, edges[d], DIRS.index((-da, -db)))
        last += [pltpu.make_async_copy(dst, src, osem.at[d, n]) for n, (src, dst) in enumerate(views)]
    for copy in last:
        copy.start()
    for p in range(2):
        for t in range(LANE_TILES):
            @pl.loop(0, TILE // PATCH)
            def _(i):
                rows = pl.ds(pl.multiple_of(HALF + i * PATCH, HALF), PATCH)
                ob[p, t + 1, rows, :] += step_object * gr[p, t + 1, rows, :]
            copy = pltpu.make_async_copy(
                ob.at[p, t + 1, HALF:HALF + TILE, :], out.at[p, :, t * PATCH:(t + 1) * PATCH], sem.at[p * 8 + t])
            copy.start()
            last.append(copy)
    for copy in last:
        copy.wait()


def run_slots(positions, slot_counts, obj, ill, amplitudes, tab, terms, hearly, halo):
    dma = pltpu.SemaphoreType.DMA
    return pl.pallas_call(
        slots_kernel,
        out_shape=(f32(2, TILE, TILE),) + STRIPS + (f32(2 * PATCH, PATCH),),
        in_specs=[IN_SMEM, IN_SMEM, ANY, IN_VMEM, ANY, IN_VMEM, ANY, IN_VMEM] + [ANY] * 8,
        out_specs=(ANY,) * 9 + (IN_VMEM,),
        scratch_shapes=[
            pltpu.VMEM((2, LANE_TILES + 3, TILE + PATCH, PATCH), jnp.float32),
            pltpu.VMEM((2, LANE_TILES + 2, TILE + PATCH, PATCH), jnp.float32),
            pltpu.VMEM((2 * PATCH, PATCH), jnp.float32), pltpu.VMEM((CAP, PATCH, PATCH), jnp.float32),
            pltpu.VMEM((RING, 2, PATCH, PATCH), jnp.float32), pltpu.SMEM((CAP,), jnp.int32), pltpu.SMEM((CAP,), jnp.int32),
            dma((16,)), dma((CAP,)), dma((RING,)), dma((8, 16)),
        ],
        compiler_params=pltpu.CompilerParams(vmem_limit_bytes=58 * 2**20),
    )(positions, slot_counts, obj, ill, amplitudes, tab, terms, hearly, *halo)


def return_kernel(h, *refs):
    edges, strips, total = refs[:8], refs[8:16], refs[16]
    other, mine, pieces, sums, gathered, send_sem, recv_sem, s0, r0, s1, r1, s2, r2, s3, r3 = refs[17:]
    a, b, rows, cols = place()
    chips = cols // 2
    q, core = b // 2, lax.rem(b, 2)
    partner = (a, b + 1 - 2 * core)

    def row_peer(k):
        return lax.rem(a + k, rows)

    def chip_peer(k):
        return lax.rem(q + k, chips)

    barrier = pltpu.get_barrier_semaphore()
    greet_strips(barrier, DIRS[4:])
    pl.semaphore_signal(barrier, inc=1, device_id=partner, device_id_type=MESH)
    for k in range(1, rows):
        pl.semaphore_signal(barrier, inc=1, device_id=(row_peer(k), b), device_id_type=MESH)
    for k in range(1, chips):
        pl.semaphore_signal(barrier, inc=1, device_id=(a, chip_peer(k) * 2 + core), device_id_type=MESH)
    across = ((core == 1) & (b < cols - 1)) | ((core == 0) & (b > 0))
    side = b + 2 * core - 1

    @pl.when(across)
    def _():
        pl.semaphore_signal(barrier, inc=1, device_id=(a, side), device_id_type=MESH)
    high = (a > 0).astype(jnp.int32) + (a < rows - 1).astype(jnp.int32)
    wide = (b > 0).astype(jnp.int32) + (b < cols - 1).astype(jnp.int32)
    pl.semaphore_wait(barrier, 1 + rows - 1 + chips - 1 + across.astype(jnp.int32) + high * wide)

    def piece_rows(k):
        return pl.ds(pl.multiple_of(k * SMALL_ROWS, SMALL_ROWS), SMALL_ROWS)

    def half_rows(k):
        return pl.ds(pl.multiple_of(k * PATCH, PATCH), PATCH)

    def remote(src, dst, send, recv, device):
        return pltpu.make_async_remote_copy(
            src_ref=src, dst_ref=dst, send_sem=send, recv_sem=recv, device_id=device, device_id_type=MESH)

    def swap():
        return remote(h.at[half_rows(1 - core)], other, s0.at[0], r0.at[0], partner)

    def scatter(peer, slot):
        return remote(mine.at[piece_rows(peer)], pieces.at[slot], s1.at[peer], r1.at[slot], (peer, b))

    def share(peer, slot):
        return remote(sums.at[slot], sums.at[slot], s2.at[peer], r2.at[slot], (a, peer * 2 + core))

    def gather(peer, slot):
        return remote(gathered.at[core, slot], gathered.at[core, slot], s3.at[peer], r3.at[slot], (peer, b))

    def hand(which):
        return remote(gathered.at[which], gathered.at[which], s0.at[1], r0.at[1], partner)

    def parts(refs, c):
        return [
            ref if d >= 4 else ref.at[:, c * (HALF // CHUNKS):(c + 1) * (HALF // CHUNKS), :] if d < 2
            else ref.at[:, c * (TILE // 2 // CHUNKS):(c + 1) * (TILE // 2 // CHUNKS), :]
            for d, ref in enumerate(refs)
        ]

    def send_strips(stage):
        for c in range(PACE[stage], PACE[stage + 1]):
            start_strips(parts(edges, c), parts(strips, c), send_sem.at[c], recv_sem.at[c], range(8) if c == 0 else range(4))

    swap().start()
    send_strips(0)
    swap().wait_recv()
    mine[...] = h[half_rows(core), :] + other[...]
    for k in range(1, rows):
        scatter(row_peer(k), a).start()
    send_strips(1)
    pieces[a] = mine[piece_rows(a), :]
    for k in range(1, rows):
        scatter(a, row_peer(k)).wait_recv()
    sums[q] = jnp.sum(pieces[...], axis=0)
    for k in range(1, chips):
        share(chip_peer(k), q).start()
    send_strips(2)
    for k in range(1, chips):
        share(q, chip_peer(k)).wait_recv()
    gathered[core, a] = jnp.sum(sums[...], axis=0)
    for k in range(1, rows):
        gather(row_peer(k), a).start()
    send_strips(3)
    for k in range(1, rows):
        gather(a, row_peer(k)).wait_recv()
    hand(core).start()
    hand(1 - core).wait_recv()
    total[...] = gathered[...]
    swap().wait_send()
    hand(core).wait_send()
    for k in range(1, rows):
        scatter(row_peer(k), a).wait_send()
        gather(row_peer(k), a).wait_send()
    for k in range(1, chips):
        share(chip_peer(k), q).wait_send()
    for c in range(CHUNKS):
        wait_strips(parts(edges, c), parts(strips, c), send_sem.at[c], recv_sem.at[c], range(8) if c == 0 else range(4))


def return_edges(h, edges):
    rows, chips = lax.axis_size("row"), lax.axis_size("col") // 2
    dma = pltpu.SemaphoreType.DMA
    return pl.pallas_call(
        return_kernel,
        out_shape=STRIPS + (f32(2, rows, SMALL_ROWS, PATCH),),
        in_specs=[IN_VMEM] + [ANY] * 8,
        out_specs=(ANY,) * 8 + (IN_VMEM,),
        scratch_shapes=[
            pltpu.VMEM((PATCH, PATCH), jnp.float32), pltpu.VMEM((PATCH, PATCH), jnp.float32),
            pltpu.VMEM((rows, SMALL_ROWS, PATCH), jnp.float32), pltpu.VMEM((chips, SMALL_ROWS, PATCH), jnp.float32),
            pltpu.VMEM((2, rows, SMALL_ROWS, PATCH), jnp.float32), dma((CHUNKS, 8)), dma((CHUNKS, 8)),
            dma((2,)), dma((2,)), dma((rows,)), dma((rows,)), dma((chips,)), dma((chips,)), dma((rows,)), dma((rows,)),
        ],
        compiler_params=pltpu.CompilerParams(collective_id=1, has_side_effects=True, vmem_limit_bytes=58 * 2**20),
    )(h, *edges)


def finish_kernel(rate, core, ill, total, *refs):
    strips, out, probe = refs[:8], refs[8], refs[9]
    top, bottom, west, east, sem, strip_sem = refs[10:16]
    held = refs[16:]
    middle = slice(HALF, TILE - HALF)
    parts = (
        (top, out.at[:, 0:HALF, :]), (bottom, out.at[:, TILE - HALF:TILE, :]),
        (west, out.at[:, middle, 0:PATCH]), (east, out.at[:, middle, TILE - PATCH:TILE]),
    )
    reads = [pltpu.make_async_copy(hbm, vmem, sem.at[n]) for n, (vmem, hbm) in enumerate(parts)]
    writes = [pltpu.make_async_copy(vmem, hbm, sem.at[n]) for n, (vmem, hbm) in enumerate(parts)]
    fetches = [pltpu.make_async_copy(strips[d], held[d], strip_sem.at[d]) for d in range(8)]
    for d, (da, db) in enumerate(DIRS):
        @pl.when(exists(-da, -db))
        def _():
            fetches[d].start()
    for copy in reads:
        copy.start()
    probe[...] = ill[...] + rate * total[...]
    half = TILE // 2

    def add(d):
        da, db = DIRS[d]

        @pl.when(exists(-da, -db))
        def _():
            fetches[d].wait()
            if da != 0:
                target = top if da > 0 else bottom
                cols = {0: slice(0, TILE), 1: slice(0, PATCH), -1: slice(TILE - PATCH, TILE)}[db]
                target[:, :, cols] += step_object * held[d][...]
            else:
                side = west if db > 0 else east
                cols = slice(0, PATCH) if db > 0 else slice(TILE - PATCH, TILE)
                low = lax.broadcasted_iota(jnp.int32, (half, PATCH), 1) < HALF
                keep = low if db > 0 else jnp.logical_not(low)
                for p in range(2):
                    first = jnp.where(keep, step_object * held[d][p], 0.0)
                    second = jnp.where(keep, pltpu.roll(step_object * held[d][p], HALF, 1), 0.0)
                    top[p, :, cols] += first[0:HALF]
                    side[p, 0:half - HALF, :] += first[HALF:half]
                    side[p, half - HALF:TILE - PATCH, :] += second[0:half - HALF]
                    bottom[p, :, cols] += second[half - HALF:half]

    for n in (0, 1, 2):
        reads[n].wait()
    add(2)
    writes[2].start()
    reads[3].wait()
    add(3)
    writes[3].start()
    for d in (0, 4, 5):
        add(d)
    writes[0].start()
    for d in (1, 6, 7):
        add(d)
    writes[1].start()
    for copy in writes:
        copy.wait()


def finish(core, ill, total, strips):
    rate = (CAP * lax.axis_size("row") * lax.axis_size("col")) ** (-0.5)
    return pl.pallas_call(
        functools.partial(finish_kernel, rate),
        out_shape=(f32(2, TILE, TILE), f32(2, PATCH, PATCH)),
        in_specs=[ANY, IN_VMEM, IN_VMEM] + [ANY] * 8,
        out_specs=(ANY, IN_VMEM),
        input_output_aliases={0: 0},
        scratch_shapes=[
            pltpu.VMEM((2, HALF, TILE), jnp.float32), pltpu.VMEM((2, HALF, TILE), jnp.float32),
            pltpu.VMEM((2, TILE - PATCH, PATCH), jnp.float32), pltpu.VMEM((2, TILE - PATCH, PATCH), jnp.float32),
            pltpu.SemaphoreType.DMA((4,)), pltpu.SemaphoreType.DMA((8,)),
        ] + [pltpu.VMEM(strip.shape, jnp.float32) for strip in STRIPS],
        compiler_params=pltpu.CompilerParams(vmem_limit_bytes=58 * 2**20),
    )(core, ill, total.reshape(2, PATCH, PATCH), *strips)


def shards(object_field, illumination, positions, slot_counts, amplitudes):
    shared = (jnp.swapaxes(positions, 2, 3), slot_counts, object_field, illumination, amplitudes, jnp.asarray(tables()))
    *halo, terms, hearly = run_early(*shared)
    core, *rest = run_slots(*shared, terms, hearly, halo)
    edges, h = rest[:8], rest[8]
    *strips, total = return_edges(h, edges)
    return finish(core, illumination, total, strips)


def solution(mesh):
    placed = (
        P(None, "row", "col"),
        P(),
        P("row", "col", None, None),
        P("row", "col"),
        P("row", "col", None, None, None),
    )
    return jax.shard_map(
        shards, mesh=mesh, in_specs=placed, out_specs=(P(None, "row", "col"), P()), check_vma=False
    )
```
